128 devices in a mesh: ctx: 16 (over z, x_hi, core), fsdp: 8 (over x_lo, y).
Axes of the slice: x: 4 (x_hi: 2, x_lo: 2; x = x_hi * 2 + x_lo), y: 4, z: 4, core: 2. Of those that a mesh axis runs over, the one named last changes fastest.
Arguments:
- tokens: bfloat16 [8, 2048, 1024], P('fsdp', 'ctx'), may hold values from -6 to 6
- w_qkv: bfloat16 [1024, 3072], P('fsdp'), may hold values from -0.25 to 0.25
- w_out: bfloat16 [1024, 1024], P('fsdp'), may hold values from -0.75 to 0.75
- w_up: bfloat16 [1024, 4096], P('fsdp'), may hold values from -0.1875 to 0.1875
- w_down: bfloat16 [1024, 4096], P('fsdp'), may hold values from -0.125 to 0.125
- ln1_gain: bfloat16 [1024], P('fsdp'), may hold values from 0.5 to 1.5
- ln1_bias: bfloat16 [1024], P('fsdp'), may hold values from -2.5 to 2.5
- ln2_gain: bfloat16 [1024], P('fsdp'), may hold values from 0.5 to 1.5
- ln2_bias: bfloat16 [1024], P('fsdp'), may hold values from -2.5 to 2.5
- cotangent: bfloat16 [8, 2048, 1024], P('fsdp', 'ctx'), may hold values from -6 to 6
Outputs:
- layer_out: bfloat16 [8, 2048, 1024], P('fsdp', 'ctx')
- input_grad: float32 [8, 2048, 1024], P('fsdp', 'ctx')
- grad_w_qkv: float32 [1024, 3072], P('fsdp')
- grad_w_out: float32 [1024, 1024], P('fsdp')
- grad_w_up: float32 [1024, 4096], P('fsdp')
- grad_w_down: float32 [1024, 4096], P('fsdp')
- grad_ln1_gain: float32 [1024], P('fsdp')
- grad_ln1_bias: float32 [1024], P('fsdp')
- grad_ln2_gain: float32 [1024], P('fsdp')
- grad_ln2_bias: float32 [1024], P('fsdp')
The draws below stay inside these ranges and needn't reach their ends.
All inputs are finite; a program needn't handle non-finite values.
Results may differ from the reference program's by a relative error of at most 0.023.
Values may be sent and summed in bfloat16 or wider, within the bound.
No kernel may reach another device: no remote copies, remote signals or barrier semaphores. Data moves between devices by JAX's collectives and lax.ppermute only.
A program may use at most 256 MiB of HBM per device.

```python
import math
import jax
import jax.numpy as jnp
from jax import lax

D = 1024
HEADS = 16
HEAD_DIM = 64
FF = 4096
LENGTH = 2048
SEQS = 8


def level_of(stream_key, extent, pieces, low, top_value):
    gain = 1.0
    for position, shards_of in pieces:
        draws = jax.random.uniform(jax.random.fold_in(jax.random.fold_in(stream_key, 6), position), (shards_of,), jnp.float32, low / len(pieces), top_value / len(pieces))
        gain = gain * jnp.repeat(jnp.exp(draws), extent[position] // shards_of).reshape((-1,) + (1,) * (len(extent) - 1 - position))
    return gain


def noise(stream_key, extent, scale, reach, split=(), held_as=jnp.bfloat16):
    values = jax.random.normal(stream_key, extent, jnp.float32) * scale
    if len(split) > 0:
        values = level_of(stream_key, extent, split, -0.22, 0.18) * values
    return jnp.clip(values, min=-reach, max=reach).astype(held_as)


def setup_inputs(seed: int = 0) -> dict:
    streams_of = jax.random.split(jax.random.key(seed), 11)
    return {
        "tokens": noise(streams_of[0], (SEQS, LENGTH, D), 1.0, 6.0, ((0, 8), (1, 16))),
        "w_qkv": noise(streams_of[1], (D, 3 * D), (D // 2) ** -0.5, 0.25, ((0, 8),)),
        "w_out": noise(streams_of[2], (D, D), (D // 16) ** -0.5, 0.75, ((0, 8),)),
        "w_up": noise(streams_of[3], (D, FF), D ** -0.5, 0.1875, ((0, 8),)),
        "w_down": noise(streams_of[4], (D, FF), (FF // 2) ** -0.5, 0.125, ((0, 8),)),
        "ln1_gain": jnp.clip(1.0 + 0.1 * jax.random.normal(streams_of[5], (D,), jnp.float32), 0.5, 1.5).astype(jnp.bfloat16),
        "ln1_bias": noise(streams_of[6], (D,), 0.5, 2.5, ((0, 8),)),
        "ln2_gain": jnp.clip(1.0 + 0.1 * jax.random.normal(streams_of[7], (D,), jnp.float32), 0.5, 1.5).astype(jnp.bfloat16),
        "ln2_bias": noise(streams_of[8], (D,), 0.5, 2.5, ((0, 8),)),
        "cotangent": noise(streams_of[9], (SEQS, LENGTH, D), 1.0, 6.0, ((0, 8), (1, 16))),
    }


@jax.custom_vjp
def low(v):
    return lax.optimization_barrier(v.astype(jnp.bfloat16)).astype(jnp.float32)

@jax.custom_vjp
def low_back(v):
    return v

def low_keep(v):
    return (low(v), None)

def low_pass(kept, grad):
    return (grad,)

def back_keep(v):
    return (v, None)

def back_low(kept, grad):
    return (low(grad),)
low.defvjp(low_keep, low_pass)
low_back.defvjp(back_keep, back_low)
epsilon = 1e-12
highest = lax.Precision.HIGHEST

def layer_norm(values, norm_gain, norm_bias):
    center = values - lax.optimization_barrier(jnp.mean(values, axis=-1, keepdims=True))
    spread = lax.optimization_barrier(jnp.mean(center * center, axis=-1, keepdims=True))
    return center * lax.rsqrt(spread + epsilon) * norm_gain + norm_bias

def matmul(left_side, right_side):
    return jnp.dot(left_side, right_side, precision=highest)

def attention(queries, keys, values):
    length = queries.shape[0]
    block_rows = math.gcd(length, 512)
    score_scale = HEAD_DIM ** (-0.5)
    query_blocks = queries.reshape(length // block_rows, block_rows, HEADS, HEAD_DIM)
    key_heads = keys.reshape(length, HEADS, HEAD_DIM)
    value_heads = values.reshape(length, HEADS, HEAD_DIM)

    def one_block(query_block):
        scores = low_back(jnp.einsum('qhd,khd->hqk', query_block, key_heads, precision=highest) * score_scale)
        row_top = lax.optimization_barrier(jnp.max(scores, axis=-1, keepdims=True))
        weights = jnp.exp(scores - row_top)
        probabilities = weights / lax.optimization_barrier(jnp.sum(weights, axis=-1, keepdims=True))
        return jnp.einsum('hqk,khd->qhd', low(probabilities), value_heads, precision=highest)
    outputs = lax.map(jax.checkpoint(one_block), query_blocks)
    return outputs.reshape(length, HEADS * HEAD_DIM)

def layer(inputs, w_qkv, w_out, w_up, w_down, gain_one, bias_one, gain_two, bias_two):
    model_width = HEADS * HEAD_DIM
    projected = low(low_back(matmul(inputs, w_qkv)))
    attended = attention(projected[:, :model_width], projected[:, model_width:2 * model_width], projected[:, 2 * model_width:])
    attended = low(low_back(attended))
    branch = low_back(matmul(attended, w_out))
    hidden = layer_norm(inputs + branch, gain_one, bias_one)
    upward = low_back(matmul(low(hidden), w_up))
    activated = low(jax.nn.gelu(upward, approximate=False))
    feed_forward = low_back(jnp.dot(activated, w_down.T, precision=highest))
    return layer_norm(hidden + feed_forward, gain_two, bias_two)

def reference(tokens, w_qkv, w_out, w_up, w_down, ln1_gain, ln1_bias, ln2_gain, ln2_bias, cotangent):
    params = tuple((member.astype(jnp.float32) for member in (w_qkv, w_out, w_up, w_down, ln1_gain, ln1_bias, ln2_gain, ln2_bias)))

    def one_sequence(totals, sequence):
        seq_tokens, seq_cotangent = sequence
        output, pullback = jax.vjp(layer, seq_tokens.astype(jnp.float32), params[0], params[1], params[2], params[3], params[4], params[5], params[6], params[7])
        gradients = pullback(seq_cotangent.astype(jnp.float32))
        totals = tuple((running + update for running, update in zip(totals, gradients[1:])))
        return (totals, (output.astype(jnp.bfloat16), gradients[0]))
    initial = tuple((jnp.zeros_like(member) for member in params))
    totals, outputs = lax.scan(one_sequence, initial, (tokens, cotangent))
    return (outputs[0], outputs[1], totals[0], totals[1], totals[2], totals[3], totals[4], totals[5], totals[6], totals[7])
```

```python
import math

import jax
import jax.numpy as jnp
from jax import lax
from jax.experimental import pallas as pl
from jax.experimental.pallas import tpu as pltpu
from jax.sharding import Mesh, PartitionSpec as P

HEADS = 16
HEAD_DIM = 64
BLOCK = 128
EPSILON = 1e-12
LOW = jnp.bfloat16
FULL = jnp.float32

CTX = ("zh", "zl", "xh", "core")
FSDP = ("xl", "y")
Z = ("zh", "zl")
SCALE = HEAD_DIM**-0.5
QUERY_BLOCK = 256
PARTS = QUERY_BLOCK // BLOCK


def dot(left, right, left_dim, right_dim):
    return lax.dot_general(
        left, right, (((left_dim,), (right_dim,)), ((), ())), preferred_element_type=FULL
    )


def swap(value, axis):
    return lax.ppermute(value, axis, [(0, 1), (1, 0)])


def exchange(value, axes, mask):
    return lax.ppermute(value, axes, [(i, i ^ mask) for i in range(4)])


def with_pair(value, axis):
    return jnp.concatenate([value, swap(value, axis)], axis=0)


def with_four(value, axes):
    moved = {mask: exchange(value, axes, mask) for mask in (1, 3, 2)}
    return jnp.concatenate([value, moved[1], moved[2], moved[3]], axis=0)


def forward_kernel(place, q_ref, k_ref, v_ref, low_ref, out_ref, log_ref, keys):
    step = pl.program_id(0)

    @pl.when(step == 0)
    def _():
        keys[...] = k_ref[...].astype(FULL).T.astype(LOW)

    queries = q_ref[...] * LOW(SCALE)
    scores = dot(keys[...], queries, 1, 0)
    top = jnp.max(scores, axis=0, keepdims=True)
    weights = jnp.exp(scores - top)
    total = jnp.sum(weights, axis=0, keepdims=True)
    attended = dot(v_ref[...], weights.astype(LOW), 1, 0) / total
    out_ref[...] = attended
    log_ref[...] = top + jnp.log(total)
    low = attended.astype(LOW)
    for part in range(PARTS):
        low_ref[place[step * PARTS + part]] = low[:, part * BLOCK : (part + 1) * BLOCK]


def attention_forward(place, projected):
    length = projected.shape[1]
    return pl.pallas_call(
        forward_kernel,
        grid_spec=pltpu.PrefetchScalarGridSpec(
            num_scalar_prefetch=1,
            grid=(length // QUERY_BLOCK,),
            in_specs=[
                pl.BlockSpec((HEAD_DIM, QUERY_BLOCK), lambda i, p: (0, i)),
                pl.BlockSpec((HEAD_DIM, length), lambda i, p: (1, 0)),
                pl.BlockSpec((HEAD_DIM, length), lambda i, p: (2, 0)),
            ],
            out_specs=[
                pl.BlockSpec((length // BLOCK, HEAD_DIM, BLOCK), lambda i, p: (0, 0, 0)),
                pl.BlockSpec((HEAD_DIM, QUERY_BLOCK), lambda i, p: (0, i)),
                pl.BlockSpec((1, QUERY_BLOCK), lambda i, p: (0, i)),
            ],
            scratch_shapes=[pltpu.VMEM((length, HEAD_DIM), LOW)],
        ),
        out_shape=[
            jax.ShapeDtypeStruct((length // BLOCK, HEAD_DIM, BLOCK), LOW),
            jax.ShapeDtypeStruct((HEAD_DIM, length), FULL),
            jax.ShapeDtypeStruct((1, length), FULL),
        ],
        compiler_params=pltpu.CompilerParams(vmem_limit_bytes=40 * 1024 * 1024),
        cost_estimate=pl.CostEstimate(
            flops=16 * length * length * HEAD_DIM,
            bytes_accessed=10 * length * HEAD_DIM,
            transcendentals=length * length,
        ),
        name="attention_forward",
    )(place, projected, projected, projected)


def backward_kernel(
    place, q_ref, k_ref, v_ref, grad_ref, out_ref, log_ref, dq_ref, dk_ref, dv_ref,
    keys, values, dk, dv,
):
    step = pl.program_id(0)

    @pl.when(step == 0)
    def _():
        keys[...] = k_ref[...].astype(FULL).T.astype(LOW)
        values[...] = v_ref[...].astype(FULL).T.astype(LOW)
        dk[...] = jnp.zeros_like(dk)
        dv[...] = jnp.zeros_like(dv)

    queries = q_ref[...] * LOW(SCALE)
    grad = jnp.concatenate([grad_ref[place[step * PARTS + p]] for p in range(PARTS)], axis=1)
    delta = jnp.sum(grad.astype(FULL) * out_ref[...], axis=0, keepdims=True)
    scores = dot(keys[...], queries, 1, 0)
    probs = jnp.exp(scores - log_ref[...])
    grad_probs = dot(values[...], grad, 1, 0)
    grad_scores = (probs * (grad_probs - delta)).astype(LOW)
    dv[...] += dot(grad, probs.astype(LOW), 1, 1)
    dk[...] += dot(queries, grad_scores, 1, 1)
    dq_ref[...] = (dot(k_ref[...], grad_scores, 1, 0) * SCALE).astype(LOW)

    @pl.when(step == pl.num_programs(0) - 1)
    def _():
        dk_ref[...] = dk[...].astype(LOW)
        dv_ref[...] = dv[...].astype(LOW)


def attention_backward(place, projected, grad_blocks, attended, log_total):
    length = projected.shape[1]
    whole = jax.ShapeDtypeStruct((HEAD_DIM, length), LOW)
    return pl.pallas_call(
        backward_kernel,
        grid_spec=pltpu.PrefetchScalarGridSpec(
            num_scalar_prefetch=1,
            grid=(length // QUERY_BLOCK,),
            in_specs=[
                pl.BlockSpec((HEAD_DIM, QUERY_BLOCK), lambda i, p: (0, i)),
                pl.BlockSpec((HEAD_DIM, length), lambda i, p: (1, 0)),
                pl.BlockSpec((HEAD_DIM, length), lambda i, p: (2, 0)),
                pl.BlockSpec((length // BLOCK, HEAD_DIM, BLOCK), lambda i, p: (0, 0, 0)),
                pl.BlockSpec((HEAD_DIM, QUERY_BLOCK), lambda i, p: (0, i)),
                pl.BlockSpec((1, QUERY_BLOCK), lambda i, p: (0, i)),
            ],
            out_specs=[
                pl.BlockSpec((HEAD_DIM, QUERY_BLOCK), lambda i, p: (0, i)),
                pl.BlockSpec((HEAD_DIM, length), lambda i, p: (0, 0)),
                pl.BlockSpec((HEAD_DIM, length), lambda i, p: (0, 0)),
            ],
            scratch_shapes=[
                pltpu.VMEM((length, HEAD_DIM), LOW),
                pltpu.VMEM((length, HEAD_DIM), LOW),
                pltpu.VMEM((HEAD_DIM, length), FULL),
                pltpu.VMEM((HEAD_DIM, length), FULL),
            ],
        ),
        out_shape=[whole, whole, whole],
        compiler_params=pltpu.CompilerParams(vmem_limit_bytes=48 * 1024 * 1024),
        cost_estimate=pl.CostEstimate(
            flops=40 * length * length * HEAD_DIM,
            bytes_accessed=20 * length * HEAD_DIM,
            transcendentals=length * length,
        ),
        name="attention_backward",
    )(place, projected, projected, projected, grad_blocks, attended, log_total)


def assemble_kernel(spots, *refs):
    pieces, (up_ref, down_ref, out_ref, norm_ref, norm_rows) = refs[:4], refs[4:]
    part = up_ref.shape[1] // 4
    out_part = out_ref.shape[1] // 4
    rows = up_ref.shape[0] // 4
    for mask in range(4):
        place = pl.ds(pl.multiple_of(spots[mask] * rows, rows), rows)
        total = jnp.zeros((rows, BLOCK), FULL)
        for which, piece in enumerate(pieces):
            group = spots[4 + which]
            wide = pl.ds(pl.multiple_of(group * part, part), part)
            narrow = pl.ds(pl.multiple_of(group * out_part, out_part), out_part)
            source = slice(mask * rows, (mask + 1) * rows)
            up_ref[place, wide] = piece[source, :part].astype(FULL)
            down_ref[place, wide] = piece[source, part : 2 * part].astype(FULL)
            out_ref[place, narrow] = piece[source, 2 * part : 2 * part + out_part].astype(FULL)
            total += piece[source, 2 * part + out_part :].astype(FULL)
        norm_rows[place, :] = total
    norm_ref[...] = norm_rows[...].T[:8]


def assemble(spots, pieces, width, units):
    shapes = [(BLOCK, units), (BLOCK, units), (BLOCK, width), (8, BLOCK)]
    return pl.pallas_call(
        assemble_kernel,
        grid_spec=pltpu.PrefetchScalarGridSpec(
            num_scalar_prefetch=1,
            grid=(1,),
            in_specs=[pl.BlockSpec(p.shape, lambda i, s: (0, 0)) for p in pieces],
            out_specs=[pl.BlockSpec(s, lambda i, s: (0, 0)) for s in shapes],
            scratch_shapes=[pltpu.VMEM((BLOCK, BLOCK), FULL)],
        ),
        out_shape=[jax.ShapeDtypeStruct(s, FULL) for s in shapes],
        compiler_params=pltpu.CompilerParams(vmem_limit_bytes=32 * 1024 * 1024),
        name="assemble",
    )(spots, *pieces)


def assemble_qkv_kernel(spots, own_ref, pair_ref, out_ref):
    rows = BLOCK // 2
    width = out_ref.shape[1] // 3
    for core, piece in enumerate((own_ref, pair_ref)):
        for z in range(4):
            lane = spots[2 + core * 4 + z] * BLOCK
            for half in range(2):
                place = pl.ds(pl.multiple_of(spots[half] * rows, rows), rows)
                source = slice((z * 2 + half) * rows, (z * 2 + half + 1) * rows)
                for which in range(3):
                    columns = pl.ds(pl.multiple_of(which * width + lane, BLOCK), BLOCK)
                    out_ref[place, columns] = piece[
                        source, which * BLOCK : (which + 1) * BLOCK
                    ].astype(FULL)


def assemble_qkv(spots, own, pair, width):
    return pl.pallas_call(
        assemble_qkv_kernel,
        grid_spec=pltpu.PrefetchScalarGridSpec(
            num_scalar_prefetch=1,
            grid=(1,),
            in_specs=[pl.BlockSpec(own.shape, lambda i, s: (0, 0))] * 2,
            out_specs=pl.BlockSpec((BLOCK, 3 * width), lambda i, s: (0, 0)),
        ),
        out_shape=jax.ShapeDtypeStruct((BLOCK, 3 * width), FULL),
        compiler_params=pltpu.CompilerParams(vmem_limit_bytes=32 * 1024 * 1024),
        name="assemble_qkv",
    )(spots, own, pair)


def norm_forward(values):
    center = values - jnp.mean(values, axis=-1, keepdims=True)
    spread = jnp.mean(center * center, axis=-1, keepdims=True)
    inverse = lax.rsqrt(spread + EPSILON)
    return center * inverse, inverse


def norm_backward(grad, normal, inverse, gain):
    scaled = grad * gain
    result = inverse * (
        scaled
        - jnp.mean(scaled, axis=-1, keepdims=True)
        - normal * jnp.mean(scaled * normal, axis=-1, keepdims=True)
    )
    return result, jnp.sum(grad * normal, axis=0), jnp.sum(grad, axis=0)


def gather_group(value):
    return with_pair(with_pair(value, "zl"), "core")


def product_group(left, right, left_dim, right_dim):
    half = left.shape[0] // 2
    theirs = swap(dot(left[half:], right, left_dim, right_dim).astype(LOW), "core")
    near = dot(left[:half], right, left_dim, right_dim) + theirs.astype(FULL)
    return near[: half // 2] + swap(near[half // 2 :].astype(LOW), "zl").astype(FULL)


def per_device(
    tokens, w_qkv, w_out, w_up, w_down, ln1_gain, ln1_bias, ln2_gain, ln2_bias, cotangent
):
    inputs = tokens[0]
    width = inputs.shape[1]
    units = w_up.shape[1]
    ff_part = units // 4
    out_part = width // 4
    z, zh, zl, xh, core = (lax.axis_index(a) for a in (Z, "zh", "zl", "xh", "core"))
    group = zl * 2 + core
    pair = z * 2 + core
    place = jnp.stack(
        [
            ((z ^ dz) * 2 + (xh ^ dx)) * 2 + (core ^ dc)
            for dx in range(2)
            for dc in range(2)
            for dz in range(4)
        ]
    ).astype(jnp.int32)

    norm_rows = jnp.pad(
        jnp.stack([ln1_gain, ln1_bias, ln2_gain, ln2_bias], axis=1), ((0, 0), (0, BLOCK - 4))
    )
    up_mine = lax.dynamic_slice_in_dim(w_up, group * ff_part, ff_part, 1)
    down_mine = lax.dynamic_slice_in_dim(w_down, group * ff_part, ff_part, 1)
    rest = lax.all_gather(
        jnp.concatenate([w_out, up_mine, down_mine, norm_rows], axis=1), FSDP, axis=0, tiled=True
    )
    qkv_mine = jnp.concatenate(
        [
            lax.dynamic_slice_in_dim(w_qkv, which * width + pair * BLOCK, BLOCK, 1)
            for which in range(3)
        ],
        axis=1,
    )
    qkv_part = lax.all_to_all(
        jnp.broadcast_to(qkv_mine[None], (8,) + qkv_mine.shape),
        FSDP,
        split_axis=0,
        concat_axis=0,
        tiled=True,
    ).reshape(width, 3 * BLOCK)
    full_out = rest[:, :width]
    up_part = rest[:, width : width + ff_part]
    down_part = rest[:, width + ff_part : width + 2 * ff_part]
    norms = rest[:, width + 2 * ff_part : width + 2 * ff_part + 4].astype(FULL).T
    gain_one, bias_one, gain_two, bias_two = (norms[i : i + 1] for i in range(4))

    near = with_pair(with_four(inputs, Z), "core")
    projected = dot(qkv_part, near, 0, 1).astype(LOW).reshape(3, 2, HEAD_DIM, 8 * BLOCK)
    mine = lax.dynamic_index_in_dim(projected, xh, 1, keepdims=False).reshape(3 * HEAD_DIM, -1)
    other = lax.dynamic_index_in_dim(projected, 1 - xh, 1, keepdims=False)
    head = jnp.concatenate([mine, swap(other.reshape(3 * HEAD_DIM, -1), "xh")], axis=1)

    low_blocks, attended, log_total = attention_forward(place, head)
    attended_low = lax.all_to_all(low_blocks, CTX, split_axis=0, concat_axis=0, tiled=True)
    attended_low = (
        attended_low.reshape(4, 2, 2, HEAD_DIM, BLOCK)
        .transpose(0, 2, 1, 3, 4)
        .reshape(width, BLOCK)
    )

    residual = inputs.astype(FULL) + dot(attended_low, full_out, 0, 0)
    normal_one, inverse_one = norm_forward(residual)
    hidden = normal_one * gain_one + bias_one
    hidden_low = gather_group(hidden.astype(LOW))
    upward = dot(hidden_low, up_part, 1, 0)
    cdf = 0.5 * (1.0 + lax.erf(upward * math.sqrt(0.5)))
    pdf = jnp.exp(-0.5 * upward * upward) * (1.0 / math.sqrt(2.0 * math.pi))
    activated_low = (upward * cdf).astype(LOW)
    slope = cdf + upward * pdf
    mixed = hidden + product_group(activated_low, down_part, 1, 1)
    normal_two, inverse_two = norm_forward(mixed)
    layer_out = (normal_two * gain_two + bias_two).astype(LOW)

    grad_mixed, gain_two_grad, bias_two_grad = norm_backward(
        cotangent[0].astype(FULL), normal_two, inverse_two, gain_two
    )
    grad_mixed_low = gather_group(grad_mixed.astype(LOW))
    grad_upward_low = (dot(grad_mixed_low, down_part, 1, 0) * slope).astype(LOW)
    grad_hidden = grad_mixed + product_group(grad_upward_low, up_part, 1, 1)
    ff_terms = jnp.concatenate(
        [dot(hidden_low, grad_upward_low, 0, 0), dot(grad_mixed_low, activated_low, 0, 0)], axis=1
    ).astype(LOW)
    ff_share = lax.psum_scatter(ff_terms, FSDP, scatter_dimension=0, tiled=True)

    grad_residual, gain_one_grad, bias_one_grad = norm_backward(
        grad_hidden, normal_one, inverse_one, gain_one
    )
    grad_residual_low = grad_residual.astype(LOW)
    grad_attended = dot(full_out, grad_residual_low, 1, 1).astype(LOW)
    grad_blocks = lax.all_to_all(
        grad_attended.reshape(4, 2, 2, HEAD_DIM, BLOCK)
        .transpose(0, 2, 1, 3, 4)
        .reshape(HEADS, HEAD_DIM, BLOCK),
        CTX,
        split_axis=0,
        concat_axis=0,
        tiled=True,
    )

    attended_group = gather_group(attended_low.reshape(1, width, BLOCK))
    residual_group = gather_group(grad_residual_low)
    residual_part = lax.dynamic_slice_in_dim(residual_group, group * out_part, out_part, 1)
    out_terms = sum(
        dot(attended_group[i], residual_part[i * BLOCK : (i + 1) * BLOCK], 1, 0) for i in range(4)
    )
    norm_terms = jnp.stack([gain_one_grad, bias_one_grad, gain_two_grad, bias_two_grad], axis=1)
    out_terms = jnp.concatenate(
        [out_terms.astype(LOW), jnp.pad(norm_terms.astype(LOW), ((0, 0), (0, BLOCK - 4)))], axis=1
    )
    out_share = lax.all_to_all(
        out_terms.reshape(8, BLOCK, -1), FSDP, split_axis=0, concat_axis=0, tiled=True
    )
    out_share = jnp.sum(out_share.astype(FULL), axis=0)

    dq, dk, dv = attention_backward(place, head, grad_blocks, attended, log_total)
    grad_head = jnp.stack([dq, dk, dv])
    mine = grad_head[:, :, : 8 * BLOCK]
    theirs = swap(grad_head[:, :, 8 * BLOCK :].reshape(3 * HEAD_DIM, -1), "xh").reshape(mine.shape)
    grad_projected = jnp.stack(
        [jnp.where(xh == 0, mine, theirs), jnp.where(xh == 0, theirs, mine)], axis=1
    ).reshape(3 * BLOCK, 8 * BLOCK)
    qkv_terms = dot(near, grad_projected, 0, 1).astype(LOW)
    half = 4 * BLOCK
    theirs = swap(dot(grad_projected[:, half:], qkv_part, 0, 1).astype(LOW), "core")
    input_near = dot(grad_projected[:, :half], qkv_part, 0, 1) + theirs.astype(FULL)
    input_grad = grad_residual + input_near[:BLOCK]
    for mask in (1, 3, 2):
        sent = input_near[mask * BLOCK : (mask + 1) * BLOCK].astype(LOW)
        input_grad = input_grad + exchange(sent, Z, mask).astype(FULL)

    late = ("zh", "xh")
    me = zh * 2 + xh
    ff_share = jnp.concatenate([ff_share, out_share.astype(LOW)], axis=1)
    ff_share = ff_share.reshape(4, BLOCK // 4, -1)
    ff_sum = lax.dynamic_index_in_dim(ff_share, me, 0, keepdims=False).astype(FULL)
    for mask in (1, 2, 3):
        sent = lax.dynamic_index_in_dim(ff_share, me ^ mask, 0, keepdims=False)
        ff_sum = ff_sum + exchange(sent, late, mask).astype(FULL)
    ff_own = with_four(ff_sum.astype(LOW), late)
    ff_zl = swap(ff_own, "zl")
    ff_core = swap(ff_own, "core")
    ff_both = swap(ff_zl, "core")
    spots = [me ^ m for m in range(4)] + [
        (zl ^ dl) * 2 + (core ^ dc) for dl, dc in ((0, 0), (1, 0), (0, 1), (1, 1))
    ]
    grad_w_up, grad_w_down, grad_w_out, norm_grads = assemble(
        jnp.stack(spots).astype(jnp.int32), [ff_own, ff_zl, ff_core, ff_both], width, units
    )

    qkv_share = lax.all_to_all(
        qkv_terms.reshape(16, BLOCK // 2, -1), ("xl", "y", "xh"), split_axis=0, concat_axis=0, tiled=True
    )
    qkv_share = jnp.sum(qkv_share.astype(FULL), axis=0).astype(LOW)
    qkv_own = with_four(with_pair(qkv_share, "xh"), Z)
    qkv_pair = swap(qkv_own, "core")
    spots = [xh, 1 - xh] + [(z ^ dz) * 2 + (core ^ dc) for dc in range(2) for dz in range(4)]
    grad_w_qkv = assemble_qkv(jnp.stack(spots).astype(jnp.int32), qkv_own, qkv_pair, width)

    return (
        layer_out[None],
        input_grad[None],
        grad_w_qkv,
        grad_w_out,
        grad_w_up,
        grad_w_down,
        norm_grads[0],
        norm_grads[1],
        norm_grads[2],
        norm_grads[3],
    )


def solution(mesh):
    fine = Mesh(mesh.devices.reshape(2, 2, 2, 2, 2, 4), ("zh", "zl", "xh", "core", "xl", "y"))
    block = P(FSDP, CTX, None)
    rows = P(FSDP, None)
    row = P(FSDP)
    return jax.shard_map(
        per_device,
        mesh=fine,
        in_specs=(block, rows, rows, rows, rows, row, row, row, row, block),
        out_specs=(block, block, rows, rows, rows, rows, row, row, row, row),
        check_vma=False,
    )
```

```python
import math

import jax
import jax.numpy as jnp
from jax import lax
from jax.experimental import pallas as pl
from jax.experimental.pallas import tpu as pltpu
from jax.sharding import Mesh, PartitionSpec as P

HEADS = 16
HEAD_DIM = 64
BLOCK = 128
EPSILON = 1e-12
LOW = jnp.bfloat16
FULL = jnp.float32

CTX = ("zh", "zl", "xh", "core")
FSDP = ("xl", "y")
Z = ("zh", "zl")
SCALE = HEAD_DIM**-0.5
QUERY_BLOCK = 256
PARTS = QUERY_BLOCK // BLOCK


def dot(left, right, left_dim, right_dim):
    return lax.dot_general(
        left, right, (((left_dim,), (right_dim,)), ((), ())), preferred_element_type=FULL
    )


def swap(value, axis):
    return lax.ppermute(value, axis, [(0, 1), (1, 0)])


def exchange(value, axes, mask):
    return lax.ppermute(value, axes, [(i, i ^ mask) for i in range(4)])


def with_pair(value, axis):
    return jnp.concatenate([value, swap(value, axis)], axis=0)


def with_four(value, axes):
    moved = {mask: exchange(value, axes, mask) for mask in (1, 3, 2)}
    return jnp.concatenate([value, moved[1], moved[2], moved[3]], axis=0)


def forward_kernel(place, q_ref, k_ref, v_ref, low_ref, out_ref, log_ref, keys):
    step = pl.program_id(0)

    @pl.when(step == 0)
    def _():
        keys[...] = k_ref[...].astype(FULL).T.astype(LOW)

    queries = q_ref[...] * LOW(SCALE)
    scores = dot(keys[...], queries, 1, 0)
    top = jnp.max(scores, axis=0, keepdims=True)
    weights = jnp.exp(scores - top)
    total = jnp.sum(weights, axis=0, keepdims=True)
    attended = dot(v_ref[...], weights.astype(LOW), 1, 0) / total
    out_ref[...] = attended
    log_ref[...] = top + jnp.log(total)
    low = attended.astype(LOW)
    for part in range(PARTS):
        low_ref[place[step * PARTS + part]] = low[:, part * BLOCK : (part + 1) * BLOCK]


def attention_forward(place, projected):
    length = projected.shape[1]
    return pl.pallas_call(
        forward_kernel,
        grid_spec=pltpu.PrefetchScalarGridSpec(
            num_scalar_prefetch=1,
            grid=(length // QUERY_BLOCK,),
            in_specs=[
                pl.BlockSpec((HEAD_DIM, QUERY_BLOCK), lambda i, p: (0, i)),
                pl.BlockSpec((HEAD_DIM, length), lambda i, p: (1, 0)),
                pl.BlockSpec((HEAD_DIM, length), lambda i, p: (2, 0)),
            ],
            out_specs=[
                pl.BlockSpec((length // BLOCK, HEAD_DIM, BLOCK), lambda i, p: (0, 0, 0)),
                pl.BlockSpec((HEAD_DIM, QUERY_BLOCK), lambda i, p: (0, i)),
                pl.BlockSpec((1, QUERY_BLOCK), lambda i, p: (0, i)),
            ],
            scratch_shapes=[pltpu.VMEM((length, HEAD_DIM), LOW)],
        ),
        out_shape=[
            jax.ShapeDtypeStruct((length // BLOCK, HEAD_DIM, BLOCK), LOW),
            jax.ShapeDtypeStruct((HEAD_DIM, length), FULL),
            jax.ShapeDtypeStruct((1, length), FULL),
        ],
        compiler_params=pltpu.CompilerParams(vmem_limit_bytes=40 * 1024 * 1024),
        cost_estimate=pl.CostEstimate(
            flops=16 * length * length * HEAD_DIM,
            bytes_accessed=10 * length * HEAD_DIM,
            transcendentals=length * length,
        ),
        name="attention_forward",
    )(place, projected, projected, projected)


def backward_kernel(
    place, q_ref, k_ref, v_ref, grad_ref, out_ref, log_ref, near_ref, far_ref, blocks_ref,
    keys, values, dk, dv,
):
    step = pl.program_id(0)

    @pl.when(step == 0)
    def _():
        keys[...] = k_ref[...].astype(FULL).T.astype(LOW)
        values[...] = v_ref[...].astype(FULL).T.astype(LOW)
        dk[...] = jnp.zeros_like(dk)
        dv[...] = jnp.zeros_like(dv)

    queries = q_ref[...] * LOW(SCALE)
    grad = jnp.concatenate([grad_ref[place[step * PARTS + p]] for p in range(PARTS)], axis=1)
    delta = jnp.sum(grad.astype(FULL) * out_ref[...], axis=0, keepdims=True)
    scores = dot(keys[...], queries, 1, 0)
    probs = jnp.exp(scores - log_ref[...])
    grad_probs = dot(values[...], grad, 1, 0)
    grad_scores = (probs * (grad_probs - delta)).astype(LOW)
    dv[...] += dot(grad, probs.astype(LOW), 1, 1)
    dk[...] += dot(queries, grad_scores, 1, 1)
    dq = (dot(k_ref[...], grad_scores, 1, 0) * SCALE).astype(LOW)
    steps = pl.num_programs(0)
    half = near_ref.shape[1]
    start = pl.multiple_of(lax.rem(step, steps // 2) * QUERY_BLOCK, QUERY_BLOCK)

    for part in range(PARTS):
        blocks_ref[place[step * PARTS + part], :HEAD_DIM] = dq[:, part * BLOCK : (part + 1) * BLOCK]

    @pl.when(step < steps // 2)
    def _():
        near_ref[:HEAD_DIM, pl.ds(start, QUERY_BLOCK)] = dq

    @pl.when(step >= steps // 2)
    def _():
        far_ref[:HEAD_DIM, pl.ds(start, QUERY_BLOCK)] = dq

    @pl.when(step == steps - 1)
    def _():
        for part, total in ((1, dk), (2, dv)):
            rows = slice(part * HEAD_DIM, (part + 1) * HEAD_DIM)
            near_ref[rows, :] = total[:, :half].astype(LOW)
            far_ref[rows, :] = total[:, half:].astype(LOW)
            for block in range(HEADS):
                blocks_ref[place[block], rows] = total[
                    :, block * BLOCK : (block + 1) * BLOCK
                ].astype(LOW)


def attention_backward(place, projected, grad_blocks, attended, log_total):
    length = projected.shape[1]
    half = jax.ShapeDtypeStruct((3 * HEAD_DIM, length // 2), LOW)
    blocks = jax.ShapeDtypeStruct((length // BLOCK, 3 * HEAD_DIM, BLOCK), LOW)
    return pl.pallas_call(
        backward_kernel,
        grid_spec=pltpu.PrefetchScalarGridSpec(
            num_scalar_prefetch=1,
            grid=(length // QUERY_BLOCK,),
            in_specs=[
                pl.BlockSpec((HEAD_DIM, QUERY_BLOCK), lambda i, p: (0, i)),
                pl.BlockSpec((HEAD_DIM, length), lambda i, p: (1, 0)),
                pl.BlockSpec((HEAD_DIM, length), lambda i, p: (2, 0)),
                pl.BlockSpec((length // BLOCK, HEAD_DIM, BLOCK), lambda i, p: (0, 0, 0)),
                pl.BlockSpec((HEAD_DIM, QUERY_BLOCK), lambda i, p: (0, i)),
                pl.BlockSpec((1, QUERY_BLOCK), lambda i, p: (0, i)),
            ],
            out_specs=[pl.BlockSpec(half.shape, lambda i, p: (0, 0))] * 2
            + [pl.BlockSpec(blocks.shape, lambda i, p: (0, 0, 0))],
            scratch_shapes=[
                pltpu.VMEM((length, HEAD_DIM), LOW),
                pltpu.VMEM((length, HEAD_DIM), LOW),
                pltpu.VMEM((HEAD_DIM, length), FULL),
                pltpu.VMEM((HEAD_DIM, length), FULL),
            ],
        ),
        out_shape=[half, half, blocks],
        compiler_params=pltpu.CompilerParams(vmem_limit_bytes=58 * 1024 * 1024),
        cost_estimate=pl.CostEstimate(
            flops=40 * length * length * HEAD_DIM,
            bytes_accessed=20 * length * HEAD_DIM,
            transcendentals=length * length,
        ),
        name="attention_backward",
    )(place, projected, projected, projected, grad_blocks, attended, log_total)


def assemble_kernel(spots, own_ref, pair_ref, up_ref, down_ref):
    part = up_ref.shape[1] // 4
    rows = up_ref.shape[0]
    for core, piece in enumerate((own_ref, pair_ref)):
        for zl in range(2):
            lane = pl.multiple_of(spots[core * 2 + zl] * part, part)
            source = slice(zl * rows, (zl + 1) * rows)
            up_ref[:, pl.ds(lane, part)] = piece[source, :part].astype(FULL)
            down_ref[:, pl.ds(lane, part)] = piece[source, part:].astype(FULL)


def assemble(spots, pieces, units):
    shape = jax.ShapeDtypeStruct((BLOCK, units), FULL)
    return local_call(assemble_kernel, spots, pieces, [shape, shape], [], "assemble")


def terms_kernel(spots, near_ref, far_ref, part_0, part_1, part_2, part_3, block_0, block_1, block_2,
                 block_3, first_ref, second_ref, out_ref, total):
    size = near_ref.shape[0]
    count = part_0.shape[0]
    length = near_ref.shape[1]
    columns = out_ref.shape[1] - size - 16
    lanes = pl.ds(pl.multiple_of(spots[0] * columns, columns), columns)
    out = jnp.zeros((columns, length), FULL)
    for block in (block_0, block_1, block_2, block_3):
        out += dot(block[:BLOCK, lanes].astype(FULL).T.astype(LOW), block[BLOCK:], 1, 0)
    total[...] = jnp.zeros_like(total)
    for index, part in enumerate((part_0, part_1, part_2, part_3)):
        source = (near_ref, far_ref)[index // 2]
        start = index % 2 * count
        total[...] += dot(source[:, start : start + count], part[...], 1, 0)
    for block in range(out_ref.shape[0]):
        rows = slice(block * BLOCK, (block + 1) * BLOCK)
        out_ref[block, :size] = total[:, rows].astype(LOW)
        out_ref[block, size : size + columns] = out[:, rows].astype(LOW)
        norms = jnp.concatenate(
            [first_ref[:, rows], second_ref[:, rows], jnp.zeros((12, BLOCK), FULL)], axis=0
        )
        out_ref[block, size + columns :] = norms.astype(LOW)


def weight_terms(spots, near, far, parts, blocks, first, second):
    size, length = near.shape
    columns = length // 4
    outs = [jax.ShapeDtypeStruct((length // BLOCK, size + columns + 16, BLOCK), LOW)]
    arrays = [near, far, *parts, *blocks, first, second]
    scratch = [pltpu.VMEM((size, length), FULL)]
    return local_call(terms_kernel, spots, arrays, outs, scratch, "weight_terms")[0]


def assemble_rest_kernel(spots, own_ref, pair_ref, qkv_ref, out_ref, norm_ref):
    width = out_ref.shape[1]
    part = width // 4
    size = 3 * HEAD_DIM
    step = own_ref.shape[0] // 2
    flip = spots[12] == 1
    total = jnp.zeros((16, BLOCK), FULL)
    for core, piece in enumerate((own_ref, pair_ref)):
        for zl in range(2):
            for zh in range(2):
                start = zl * step + zh * 2 * size
                lane = spots[(core * 2 + zl) * 2 + zh] * BLOCK
                near = piece[start : start + size].astype(FULL)
                far = piece[start + size : start + 2 * size].astype(FULL)
                first = jnp.where(flip, far, near)
                second = jnp.where(flip, near, far)
                for which in range(3):
                    rows = slice(which * HEAD_DIM, (which + 1) * HEAD_DIM)
                    columns = pl.ds(pl.multiple_of(which * width + lane, BLOCK), BLOCK)
                    qkv_ref[:, columns] = jnp.concatenate([first[rows], second[rows]], axis=0).T
            start = zl * step + 4 * size
            lane = pl.multiple_of(spots[8 + core * 2 + zl] * part, part)
            out_ref[:, pl.ds(lane, part)] = piece[start : start + part].astype(FULL).T
            total += piece[start + part : start + part + 16].astype(FULL)
    norm_ref[...] = total


def assemble_rest(spots, own, pair, width):
    outs = [
        jax.ShapeDtypeStruct((BLOCK, 3 * width), FULL),
        jax.ShapeDtypeStruct((BLOCK, width), FULL),
        jax.ShapeDtypeStruct((16, BLOCK), FULL),
    ]
    return local_call(assemble_rest_kernel, spots, [own, pair], outs, [], "assemble_rest")


def input_kernel(spots, every_ref, own_ref, pair_ref, base_ref, out_ref, grads):
    half = own_ref.shape[1]

    @pl.when(pl.program_id(0) == 0)
    def _():
        for which in range(3):
            for head in range(HEADS):
                start = (which * HEADS + head) * HEAD_DIM
                grads[start : start + HEAD_DIM, :] = every_ref[
                    head_place(head), which * HEAD_DIM : (which + 1) * HEAD_DIM
                ]

    total = jnp.zeros((own_ref.shape[0], BLOCK), FULL)
    for core, part in enumerate((own_ref, pair_ref)):
        rows = pl.ds(pl.multiple_of(spots[core] * half, half), half)
        total += dot(part[...], grads[rows, :], 1, 0)
    out_ref[...] = base_ref[...] + total.T


def input_product(spots, every, own, pair, base):
    rows, width = base.shape
    tile = 512
    weights = pl.BlockSpec((tile, own.shape[1]), lambda i, s: (i, 0))
    block = pl.BlockSpec((rows, tile), lambda i, s: (0, i))
    return pl.pallas_call(
        input_kernel,
        grid_spec=pltpu.PrefetchScalarGridSpec(
            num_scalar_prefetch=1,
            grid=(width // tile,),
            in_specs=[pl.BlockSpec(every.shape, lambda i, s: (0, 0, 0)), weights, weights, block],
            out_specs=block,
            scratch_shapes=[pltpu.VMEM((2 * own.shape[1], rows), LOW)],
        ),
        out_shape=jax.ShapeDtypeStruct((rows, width), FULL),
        compiler_params=pltpu.CompilerParams(vmem_limit_bytes=58 * 1024 * 1024),
        name="input_product",
    )(spots, every, own, pair, base)


def head_place(index):
    return (index // 4) * 4 + (index % 2) * 2 + (index // 2) % 2


def out_kernel(spots, att_ref, out_ref, x_ref, norms_ref, att_out_ref, low_ref, hid_ref,
               normal_ref, inverse_ref, rows_scratch):
    for head in range(HEADS):
        rows_scratch[head * HEAD_DIM : (head + 1) * HEAD_DIM, :] = att_ref[head_place(head)]
    attended = rows_scratch[...].astype(FULL).T.astype(LOW)
    att_out_ref[...] = attended
    residual = x_ref[...].astype(FULL) + dot(attended, out_ref[...], 1, 0)
    normal, inverse = norm_forward(residual)
    hidden = normal * norms_ref[0:1] + norms_ref[1:2]
    hid_ref[...] = hidden
    low_ref[...] = hidden.astype(LOW)
    normal_ref[...] = normal
    inverse_ref[...] = jnp.broadcast_to(inverse, (BLOCK, BLOCK))


def whole_specs(shapes):
    return [pl.BlockSpec(s, lambda i, p, n=len(s): (0,) * n) for s in shapes]


def local_call(kernel, spots, arrays, outs, scratch, name, specs=None, limit=40):
    return pl.pallas_call(
        kernel,
        grid_spec=pltpu.PrefetchScalarGridSpec(
            num_scalar_prefetch=1,
            grid=(1,),
            in_specs=specs or whole_specs([a.shape for a in arrays]),
            out_specs=whole_specs([o.shape for o in outs]),
            scratch_shapes=scratch,
        ),
        out_shape=outs,
        compiler_params=pltpu.CompilerParams(vmem_limit_bytes=limit * 1024 * 1024),
        name=name,
    )(spots, *arrays)


def out_last(arrays, index):
    specs = whole_specs([a.shape for a in arrays])
    width = arrays[index].shape[0]
    last = arrays[index].shape[1] // width - 1
    specs[index] = pl.BlockSpec((width, width), lambda i, p: (0, last))
    return specs


def out_and_norm(spots, blocks, rest, inputs, norms):
    rows, width = inputs.shape
    arrays = [blocks, rest, inputs, norms]
    shape = jax.ShapeDtypeStruct
    return local_call(
        out_kernel,
        spots,
        arrays,
        [
            shape((rows, width), LOW),
            shape((rows, width), LOW),
            shape((rows, width), FULL),
            shape((rows, width), FULL),
            shape((rows, BLOCK), FULL),
        ],
        [pltpu.VMEM((width, rows), LOW)],
        "out_and_norm",
        out_last(arrays, 1),
        58,
    )


def norm_one_kernel(spots, base_ref, late_ref, normal_ref, inverse_ref, norms_ref, out_ref,
                    grad_ref, low_ref, blocks_ref, sums_ref, total):
    grad = base_ref[...] + late_ref[...].astype(FULL)
    normal = normal_ref[...]
    result, gain_sum, bias_sum = norm_backward(grad, normal, inverse_ref[:, :1], norms_ref[0:1])
    grad_ref[...] = result
    low_ref[...] = result.astype(LOW)
    sums_ref[0:1, :] = gain_sum[None]
    sums_ref[1:2, :] = bias_sum[None]
    total[...] = dot(out_ref[...], low_ref[...], 1, 1)
    for head in range(HEADS):
        rows = slice(head * HEAD_DIM, (head + 1) * HEAD_DIM)
        blocks_ref[head_place(head)] = total[rows, :].astype(LOW)


def norm_one_back(spots, base, late, normal, inverse, norms, rest):
    rows, width = base.shape
    arrays = [base, late, normal, inverse, norms, rest]
    shape = jax.ShapeDtypeStruct
    return local_call(
        norm_one_kernel,
        spots,
        arrays,
        [
            shape((rows, width), FULL),
            shape((rows, width), LOW),
            shape((HEADS, HEAD_DIM, rows), LOW),
            shape((2, width), FULL),
        ],
        [pltpu.VMEM((width, rows), FULL)],
        "norm_one_back",
        out_last(arrays, 5),
        58,
    )


def ff_terms_kernel(hid_a, hid_b, up_a, up_b, mixed_a, mixed_b, act_a, act_b, out_ref, left):
    step = pl.program_id(0)
    steps = pl.num_programs(0) // 2
    half = hid_a.shape[0]

    @pl.when(step == 0)
    def _():
        left[:, :half] = hid_a[...].astype(FULL).T.astype(LOW)
        left[:, half:] = hid_b[...].astype(FULL).T.astype(LOW)

    @pl.when(step == steps)
    def _():
        left[:, :half] = mixed_a[...].astype(FULL).T.astype(LOW)
        left[:, half:] = mixed_b[...].astype(FULL).T.astype(LOW)

    @pl.when(step < steps)
    def _():
        right = jnp.concatenate([up_a[...], up_b[...]], axis=0)
        out_ref[...] = dot(left[...], right, 1, 0).astype(LOW)

    @pl.when(step >= steps)
    def _():
        right = jnp.concatenate([act_a[...], act_b[...]], axis=0)
        out_ref[...] = dot(left[...], right, 1, 0).astype(LOW)


def ff_products(hidden, grad_upward, grad_mixed, activated):
    count, width = hidden[0].shape
    units = activated[0].shape[1]
    tile = 512
    steps = units // tile
    whole = pl.BlockSpec((count, width), lambda i: (0, 0))
    early = pl.BlockSpec((count, tile), lambda i: (0, jnp.minimum(i, steps - 1)))
    later = pl.BlockSpec((count, tile), lambda i: (0, jnp.maximum(i - steps, 0)))
    return pl.pallas_call(
        ff_terms_kernel,
        grid=(2 * steps,),
        in_specs=[whole, whole, early, early, whole, whole, later, later],
        out_specs=pl.BlockSpec((width, tile), lambda i: (0, i)),
        out_shape=jax.ShapeDtypeStruct((width, 2 * units), LOW),
        scratch_shapes=[pltpu.VMEM((width, 2 * count), LOW)],
        compiler_params=pltpu.CompilerParams(vmem_limit_bytes=58 * 1024 * 1024),
        cost_estimate=pl.CostEstimate(
            flops=8 * count * width * units, bytes_accessed=8 * width * units, transcendentals=0
        ),
        name="ff_products",
    )(*hidden, *grad_upward, *grad_mixed, *activated)


def norm_forward(values):
    center = values - jnp.mean(values, axis=-1, keepdims=True)
    spread = jnp.mean(center * center, axis=-1, keepdims=True)
    inverse = lax.rsqrt(spread + EPSILON)
    return center * inverse, inverse


def norm_backward(grad, normal, inverse, gain):
    scaled = grad * gain
    result = inverse * (
        scaled
        - jnp.mean(scaled, axis=-1, keepdims=True)
        - normal * jnp.mean(scaled * normal, axis=-1, keepdims=True)
    )
    return result, jnp.sum(grad * normal, axis=0), jnp.sum(grad, axis=0)


def gather_group(value):
    late = swap(value, "zl")
    near = with_pair(value, "core")
    return near, with_pair(late, "core")


def product_group(parts, right, left_dim, right_dim):
    near, far = parts
    half = far.shape[0] // 2
    term = dot(far, right, left_dim, right_dim)
    sent = term[:half] + swap(term[half:].astype(LOW), "core").astype(FULL)
    sent, near = lax.optimization_barrier((sent.astype(LOW), near))
    late = swap(sent, "zl")
    term = dot(near, right, left_dim, right_dim)
    return term[:half] + swap(term[half:].astype(LOW), "core").astype(FULL), late, sent


def per_device(
    tokens, w_qkv, w_out, w_up, w_down, ln1_gain, ln1_bias, ln2_gain, ln2_bias, cotangent
):
    inputs = tokens[0]
    width = inputs.shape[1]
    units = w_up.shape[1]
    ff_part = units // 4
    out_part = width // 4
    z, zh, zl, xh, core = (lax.axis_index(a) for a in (Z, "zh", "zl", "xh", "core"))
    group = zl * 2 + core
    pair = z * 2 + core
    place = jnp.stack(
        [
            ((z ^ dz) * 2 + (xh ^ dx)) * 2 + (core ^ dc)
            for dx in range(2)
            for dc in range(2)
            for dz in (0, 1, 3, 2)
        ]
    ).astype(jnp.int32)
    cores = jnp.stack([core, 1 - core]).astype(jnp.int32)
    groups = jnp.stack(
        [(zl ^ dl) * 2 + (core ^ dc) for dc in range(2) for dl in range(2)]
    ).astype(jnp.int32)

    heads = [
        lax.dynamic_slice_in_dim(w_qkv, which * width + pair * BLOCK, BLOCK, 1) for which in range(3)
    ]
    first = jnp.concatenate([h[:, :HEAD_DIM] for h in heads], axis=1)
    second = jnp.concatenate([h[:, HEAD_DIM:] for h in heads], axis=1)
    own_mine = jnp.where(xh == 0, first, second)
    norm_rows = jnp.pad(
        jnp.stack([ln1_gain, ln1_bias, ln2_gain, ln2_bias]), ((0, 12), (0, BLOCK))
    )
    early = jnp.concatenate([jnp.pad(own_mine, ((0, 0), (0, HEAD_DIM))), norm_rows], axis=0)
    together = lax.optimization_barrier
    early, inputs = together((jnp.broadcast_to(early[None], (8,) + early.shape), inputs))
    early = lax.all_to_all(early, FSDP, split_axis=0, concat_axis=0, tiled=True)
    up_mine = lax.dynamic_slice_in_dim(w_up, group * ff_part, ff_part, 1)
    down_mine = lax.dynamic_slice_in_dim(w_down, group * ff_part, ff_part, 1)
    rest = jnp.concatenate([up_mine, down_mine, w_out], axis=1)
    rest = lax.all_gather(rest, FSDP, axis=0, tiled=True)
    far, one = together((swap(inputs, "xh"), exchange(inputs, Z, 1)))
    near_two = jnp.concatenate([inputs, one], axis=0)
    near_rest, far_one = together((exchange(near_two, Z, 3), exchange(far, Z, 1)))
    near_half, early = together((jnp.concatenate([near_two, near_rest], axis=0), early))
    far_two = jnp.concatenate([far, far_one], axis=0)
    far_rest = exchange(far_two, Z, 3)
    near_core = swap(near_half, "core")
    far_half = jnp.concatenate([far_two, far_rest], axis=0)
    parts = [near_half, near_core, far_half, swap(far_half, "core")]
    own_qkv = early[:, :BLOCK, : 3 * HEAD_DIM].reshape(width, 3 * HEAD_DIM)
    norms = early[:, BLOCK : BLOCK + 4, :BLOCK].astype(FULL).transpose(1, 0, 2).reshape(4, width)
    gain_two, bias_two = norms[2:3], norms[3:4]
    head = jnp.concatenate([dot(own_qkv, p, 0, 1).astype(LOW) for p in parts], axis=1)

    low_blocks, attended, log_total = attention_forward(place, head)
    low_blocks = lax.all_to_all(low_blocks, CTX, split_axis=0, concat_axis=0, tiled=True)
    qkv_mine = lax.dynamic_slice_in_dim(w_qkv, core * (3 * width // 2), 3 * width // 2, 1)
    rest, qkv_mine, low_blocks = together((rest, qkv_mine, low_blocks))
    up_part = rest[:, :ff_part]
    down_part = rest[:, ff_part : 2 * ff_part]
    qkv_own = lax.all_gather(qkv_mine, FSDP, axis=0, tiled=True)
    attended_low, hidden_low, hidden, normal_one, inverse_one = out_and_norm(
        cores, low_blocks, rest, inputs, norms
    )
    hidden_low = gather_group(hidden_low)
    upward = [dot(h, up_part, 1, 0) for h in hidden_low]
    cdf = [0.5 * (1.0 + lax.erf(u * math.sqrt(0.5))) for u in upward]
    activated_low = [(u * c).astype(LOW) for u, c in zip(upward, cdf)]
    slope = [
        c + u * jnp.exp(-0.5 * u * u) * (1.0 / math.sqrt(2.0 * math.pi))
        for u, c in zip(upward, cdf)
    ]
    near, late, _ = product_group(activated_low, down_part, 1, 1)
    mixed = hidden + near + late.astype(FULL)
    normal_two, inverse_two = norm_forward(mixed)
    layer_out = (normal_two * gain_two + bias_two).astype(LOW)

    grad_mixed, gain_two_grad, bias_two_grad = norm_backward(
        cotangent[0].astype(FULL), normal_two, inverse_two, gain_two
    )
    grad_mixed_low = gather_group(grad_mixed.astype(LOW))
    grad_upward_low = [
        (dot(g, down_part, 1, 0) * k).astype(LOW) for g, k in zip(grad_mixed_low, slope)
    ]
    near, late, sent = product_group(grad_upward_low, up_part, 1, 1)
    late, qkv_own = together((late, qkv_own))
    qkv_pair = swap(qkv_own, "core")
    near, *held = together((near, *hidden_low))
    ff_terms = ff_products(held, grad_upward_low, grad_mixed_low, activated_low)
    ff_share = lax.psum_scatter(ff_terms, FSDP, scatter_dimension=0, tiled=True)

    grad_residual, grad_residual_low, grad_blocks, norm_one_sums = norm_one_back(
        cores, grad_mixed + near, late, normal_one, inverse_one, norms, rest
    )
    grad_blocks = lax.all_to_all(grad_blocks, CTX, split_axis=0, concat_axis=0, tiled=True)
    pairs = jnp.concatenate([grad_residual_low, attended_low], axis=0)
    late_pairs = swap(pairs, "zl")
    blocks = [pairs, swap(pairs, "core"), late_pairs, swap(late_pairs, "core")]

    grad_near, grad_far, grad_out = attention_backward(
        place, head, grad_blocks, attended, log_total
    )
    norm_two_sums = jnp.stack([gain_two_grad, bias_two_grad])
    terms = weight_terms(
        groups[:1], grad_near, grad_far, parts, blocks, norm_one_sums, norm_two_sums
    )
    shares = lax.all_to_all(terms, FSDP, split_axis=0, concat_axis=0, tiled=True)

    def sum_pair(value, axis):
        return (value.astype(FULL) + swap(value, axis).astype(FULL)).astype(LOW)

    size = 3 * HEAD_DIM
    def spread(qkv_part, out_part, axis):
        theirs = swap(jnp.concatenate([qkv_part, out_part], axis=0), axis)
        count = qkv_part.shape[0]
        summed = out_part.astype(FULL) + theirs[count:].astype(FULL)
        return jnp.concatenate([qkv_part, theirs[:count]], axis=0), summed.astype(LOW)

    ff_share, grad_out = together((ff_share, grad_out, terms))[:2]
    ff_sum, shares = together((sum_pair(ff_share, "zh"), shares))
    shares = jnp.sum(shares.astype(FULL), axis=0).astype(LOW)
    every = lax.all_to_all(grad_out, CTX, split_axis=0, concat_axis=0, tiled=True)
    ff_sum, every, *sums = together(
        (sum_pair(ff_sum, "xh"), every, *spread(shares[:size], shares[size:], "xh"))
    )
    input_grad = input_product(cores, every, qkv_own, qkv_pair, grad_residual)
    rest_sum = jnp.concatenate(spread(*sums, "zh"), axis=0)
    ff_sum, input_grad, rest_sum = together(
        (with_pair(ff_sum, "zl"), input_grad, with_pair(rest_sum, "zl"))
    )
    ff_pair, rest_pair = swap(ff_sum, "core"), swap(rest_sum, "core")
    spots = [
        ((zh ^ dh) * 2 + (zl ^ dl)) * 2 + (core ^ dc)
        for dc in range(2)
        for dl in range(2)
        for dh in range(2)
    ]
    spots = jnp.concatenate([jnp.stack(spots).astype(jnp.int32), groups, xh[None].astype(jnp.int32)])
    grad_w_qkv, grad_w_out, norm_grads = assemble_rest(spots, rest_sum, rest_pair, width)
    grad_w_up, grad_w_down = assemble(groups, [ff_sum, ff_pair], units)

    return (
        layer_out[None],
        input_grad[None],
        grad_w_qkv,
        grad_w_out,
        grad_w_up,
        grad_w_down,
        norm_grads[0],
        norm_grads[1],
        norm_grads[2],
        norm_grads[3],
    )


def solution(mesh):
    fine = Mesh(mesh.devices.reshape(2, 2, 2, 2, 2, 4), ("zh", "zl", "xh", "core", "xl", "y"))
    block = P(FSDP, CTX, None)
    rows = P(FSDP, None)
    row = P(FSDP)
    return jax.shard_map(
        per_device,
        mesh=fine,
        in_specs=(block, rows, rows, rows, rows, row, row, row, row, block),
        out_specs=(block, block, rows, rows, rows, rows, row, row, row, row),
        check_vma=False,
    )
```

```python
import math

import jax
import jax.numpy as jnp
from jax import lax
from jax.experimental import pallas as pl
from jax.experimental.pallas import tpu as pltpu
from jax.sharding import Mesh, PartitionSpec as P

HEADS = 16
HEAD_DIM = 64
BLOCK = 128
EPSILON = 1e-12
LOW = jnp.bfloat16
FULL = jnp.float32

CTX = ("zh", "zl", "xh", "core")
FSDP = ("xl", "y")
Z = ("zh", "zl")
SCALE = HEAD_DIM**-0.5
QUERY_BLOCK = 256
PARTS = QUERY_BLOCK // BLOCK


def dot(left, right, left_dim, right_dim):
    return lax.dot_general(
        left, right, (((left_dim,), (right_dim,)), ((), ())), preferred_element_type=FULL
    )


def swap(value, axis):
    return lax.ppermute(value, axis, [(0, 1), (1, 0)])


def exchange(value, axes, mask):
    return lax.ppermute(value, axes, [(i, i ^ mask) for i in range(4)])


def with_pair(value, axis):
    return jnp.concatenate([value, swap(value, axis)], axis=0)


def with_four(value, axes):
    moved = {mask: exchange(value, axes, mask) for mask in (1, 3, 2)}
    return jnp.concatenate([value, moved[1], moved[2], moved[3]], axis=0)


def forward_kernel(place, q_ref, k_ref, v_ref, low_ref, out_ref, log_ref, keys):
    step = pl.program_id(0)

    @pl.when(step == 0)
    def _():
        keys[...] = k_ref[...].astype(FULL).T.astype(LOW)

    queries = q_ref[...] * LOW(SCALE)
    scores = dot(keys[...], queries, 1, 0)
    top = jnp.max(scores, axis=0, keepdims=True)
    weights = jnp.exp(scores - top)
    total = jnp.sum(weights, axis=0, keepdims=True)
    attended = dot(v_ref[...], weights.astype(LOW), 1, 0) / total
    out_ref[...] = attended
    log_ref[...] = top + jnp.log(total)
    low = attended.astype(LOW)
    for part in range(PARTS):
        low_ref[place[step * PARTS + part]] = low[:, part * BLOCK : (part + 1) * BLOCK]


def attention_forward(place, projected):
    length = projected.shape[1]
    return pl.pallas_call(
        forward_kernel,
        grid_spec=pltpu.PrefetchScalarGridSpec(
            num_scalar_prefetch=1,
            grid=(length // QUERY_BLOCK,),
            in_specs=[
                pl.BlockSpec((HEAD_DIM, QUERY_BLOCK), lambda i, p: (0, i)),
                pl.BlockSpec((HEAD_DIM, length), lambda i, p: (1, 0)),
                pl.BlockSpec((HEAD_DIM, length), lambda i, p: (2, 0)),
            ],
            out_specs=[
                pl.BlockSpec((length // BLOCK, HEAD_DIM, BLOCK), lambda i, p: (0, 0, 0)),
                pl.BlockSpec((HEAD_DIM, QUERY_BLOCK), lambda i, p: (0, i)),
                pl.BlockSpec((1, QUERY_BLOCK), lambda i, p: (0, i)),
            ],
            scratch_shapes=[pltpu.VMEM((length, HEAD_DIM), LOW)],
        ),
        out_shape=[
            jax.ShapeDtypeStruct((length // BLOCK, HEAD_DIM, BLOCK), LOW),
            jax.ShapeDtypeStruct((HEAD_DIM, length), FULL),
            jax.ShapeDtypeStruct((1, length), FULL),
        ],
        compiler_params=pltpu.CompilerParams(vmem_limit_bytes=40 * 1024 * 1024),
        cost_estimate=pl.CostEstimate(
            flops=16 * length * length * HEAD_DIM,
            bytes_accessed=10 * length * HEAD_DIM,
            transcendentals=length * length,
        ),
        name="attention_forward",
    )(place, projected, projected, projected)


def backward_kernel(
    place, q_ref, k_ref, v_ref, grad_ref, out_ref, log_ref, near_ref, far_ref, blocks_ref,
    keys, values, dk, dv,
):
    step = pl.program_id(0)

    @pl.when(step == 0)
    def _():
        keys[...] = k_ref[...].astype(FULL).T.astype(LOW)
        values[...] = v_ref[...].astype(FULL).T.astype(LOW)
        dk[...] = jnp.zeros_like(dk)
        dv[...] = jnp.zeros_like(dv)

    queries = q_ref[...] * LOW(SCALE)
    grad = jnp.concatenate([grad_ref[place[step * PARTS + p]] for p in range(PARTS)], axis=1)
    delta = jnp.sum(grad.astype(FULL) * out_ref[...], axis=0, keepdims=True)
    scores = dot(keys[...], queries, 1, 0)
    probs = jnp.exp(scores - log_ref[...])
    grad_probs = dot(values[...], grad, 1, 0)
    grad_scores = (probs * (grad_probs - delta)).astype(LOW)
    dv[...] += dot(grad, probs.astype(LOW), 1, 1)
    dk[...] += dot(queries, grad_scores, 1, 1)
    dq = (dot(k_ref[...], grad_scores, 1, 0) * SCALE).astype(LOW)
    steps = pl.num_programs(0)
    half = near_ref.shape[1]
    start = pl.multiple_of(lax.rem(step, steps // 2) * QUERY_BLOCK, QUERY_BLOCK)

    for part in range(PARTS):
        blocks_ref[place[step * PARTS + part], :HEAD_DIM] = dq[:, part * BLOCK : (part + 1) * BLOCK]

    @pl.when(step < steps // 2)
    def _():
        near_ref[:HEAD_DIM, pl.ds(start, QUERY_BLOCK)] = dq

    @pl.when(step >= steps // 2)
    def _():
        far_ref[:HEAD_DIM, pl.ds(start, QUERY_BLOCK)] = dq

    @pl.when(step == steps - 1)
    def _():
        for part, total in ((1, dk), (2, dv)):
            rows = slice(part * HEAD_DIM, (part + 1) * HEAD_DIM)
            near_ref[rows, :] = total[:, :half].astype(LOW)
            far_ref[rows, :] = total[:, half:].astype(LOW)
            for block in range(HEADS):
                blocks_ref[place[block], rows] = total[
                    :, block * BLOCK : (block + 1) * BLOCK
                ].astype(LOW)


def attention_backward(place, projected, grad_blocks, attended, log_total):
    length = projected.shape[1]
    half = jax.ShapeDtypeStruct((3 * HEAD_DIM, length // 2), LOW)
    blocks = jax.ShapeDtypeStruct((length // BLOCK, 3 * HEAD_DIM, BLOCK), LOW)
    return pl.pallas_call(
        backward_kernel,
        grid_spec=pltpu.PrefetchScalarGridSpec(
            num_scalar_prefetch=1,
            grid=(length // QUERY_BLOCK,),
            in_specs=[
                pl.BlockSpec((HEAD_DIM, QUERY_BLOCK), lambda i, p: (0, i)),
                pl.BlockSpec((HEAD_DIM, length), lambda i, p: (1, 0)),
                pl.BlockSpec((HEAD_DIM, length), lambda i, p: (2, 0)),
                pl.BlockSpec((length // BLOCK, HEAD_DIM, BLOCK), lambda i, p: (0, 0, 0)),
                pl.BlockSpec((HEAD_DIM, QUERY_BLOCK), lambda i, p: (0, i)),
                pl.BlockSpec((1, QUERY_BLOCK), lambda i, p: (0, i)),
            ],
            out_specs=[pl.BlockSpec(half.shape, lambda i, p: (0, 0))] * 2
            + [pl.BlockSpec(blocks.shape, lambda i, p: (0, 0, 0))],
            scratch_shapes=[
                pltpu.VMEM((length, HEAD_DIM), LOW),
                pltpu.VMEM((length, HEAD_DIM), LOW),
                pltpu.VMEM((HEAD_DIM, length), FULL),
                pltpu.VMEM((HEAD_DIM, length), FULL),
            ],
        ),
        out_shape=[half, half, blocks],
        compiler_params=pltpu.CompilerParams(vmem_limit_bytes=58 * 1024 * 1024),
        cost_estimate=pl.CostEstimate(
            flops=40 * length * length * HEAD_DIM,
            bytes_accessed=20 * length * HEAD_DIM,
            transcendentals=length * length,
        ),
        name="attention_backward",
    )(place, projected, projected, projected, grad_blocks, attended, log_total)


def assemble_kernel(spots, own_ref, pair_ref, up_ref, down_ref):
    part = up_ref.shape[1] // 4
    rows = up_ref.shape[0]
    for core, piece in enumerate((own_ref, pair_ref)):
        for zl in range(2):
            lane = pl.multiple_of(spots[core * 2 + zl] * part, part)
            source = slice(zl * rows, (zl + 1) * rows)
            up_ref[:, pl.ds(lane, part)] = piece[source, :part].astype(FULL)
            down_ref[:, pl.ds(lane, part)] = piece[source, part:].astype(FULL)


def assemble(spots, pieces, units):
    shape = jax.ShapeDtypeStruct((BLOCK, units), FULL)
    return local_call(assemble_kernel, spots, pieces, [shape, shape], [], "assemble")


def terms_kernel(spots, near_ref, far_ref, part_0, part_1, part_2, part_3, block_0, block_1, block_2,
                 block_3, first_ref, second_ref, out_ref, total):
    size = near_ref.shape[0]
    count = part_0.shape[0]
    length = near_ref.shape[1]
    columns = out_ref.shape[1] - size - 16
    lanes = pl.ds(pl.multiple_of(spots[0] * columns, columns), columns)
    out = jnp.zeros((columns, length), FULL)
    for block in (block_0, block_1, block_2, block_3):
        out += dot(block[:BLOCK, lanes].astype(FULL).T.astype(LOW), block[BLOCK:], 1, 0)
    total[...] = jnp.zeros_like(total)
    for index, part in enumerate((part_0, part_1, part_2, part_3)):
        source = (near_ref, far_ref)[index // 2]
        start = index % 2 * count
        total[...] += dot(source[:, start : start + count], part[...], 1, 0)
    for block in range(out_ref.shape[0]):
        rows = slice(block * BLOCK, (block + 1) * BLOCK)
        out_ref[block, :size] = total[:, rows].astype(LOW)
        out_ref[block, size : size + columns] = out[:, rows].astype(LOW)
        norms = jnp.concatenate(
            [first_ref[:, rows], second_ref[:, rows], jnp.zeros((12, BLOCK), FULL)], axis=0
        )
        out_ref[block, size + columns :] = norms.astype(LOW)


def weight_terms(spots, near, far, parts, blocks, first, second):
    size, length = near.shape
    columns = length // 4
    outs = [jax.ShapeDtypeStruct((length // BLOCK, size + columns + 16, BLOCK), LOW)]
    arrays = [near, far, *parts, *blocks, first, second]
    scratch = [pltpu.VMEM((size, length), FULL)]
    return local_call(terms_kernel, spots, arrays, outs, scratch, "weight_terms")[0]


def assemble_rest_kernel(spots, own_ref, pair_ref, qkv_ref, out_ref, norm_ref):
    width = out_ref.shape[1]
    part = width // 4
    size = 3 * HEAD_DIM
    step = own_ref.shape[0] // 2
    flip = spots[12] == 1
    total = jnp.zeros((16, BLOCK), FULL)
    for core, piece in enumerate((own_ref, pair_ref)):
        for zl in range(2):
            for zh in range(2):
                start = zl * step + zh * 2 * size
                lane = spots[(core * 2 + zl) * 2 + zh] * BLOCK
                near = piece[start : start + size].astype(FULL)
                far = piece[start + size : start + 2 * size].astype(FULL)
                first = jnp.where(flip, far, near)
                second = jnp.where(flip, near, far)
                for which in range(3):
                    rows = slice(which * HEAD_DIM, (which + 1) * HEAD_DIM)
                    columns = pl.ds(pl.multiple_of(which * width + lane, BLOCK), BLOCK)
                    qkv_ref[:, columns] = jnp.concatenate([first[rows], second[rows]], axis=0).T
            start = zl * step + 4 * size
            lane = pl.multiple_of(spots[8 + core * 2 + zl] * part, part)
            out_ref[:, pl.ds(lane, part)] = piece[start : start + part].astype(FULL).T
            total += piece[start + part : start + part + 16].astype(FULL)
    norm_ref[...] = total


def assemble_rest(spots, own, pair, width):
    outs = [
        jax.ShapeDtypeStruct((BLOCK, 3 * width), FULL),
        jax.ShapeDtypeStruct((BLOCK, width), FULL),
        jax.ShapeDtypeStruct((16, BLOCK), FULL),
    ]
    return local_call(assemble_rest_kernel, spots, [own, pair], outs, [], "assemble_rest")


def input_kernel(spots, every_ref, own_ref, pair_ref, base_ref, out_ref, grads):
    half = own_ref.shape[1]

    @pl.when(pl.program_id(0) == 0)
    def _():
        for which in range(3):
            for head in range(HEADS):
                start = (which * HEADS + head) * HEAD_DIM
                grads[start : start + HEAD_DIM, :] = every_ref[
                    head_place(head), which * HEAD_DIM : (which + 1) * HEAD_DIM
                ]

    total = jnp.zeros((own_ref.shape[0], BLOCK), FULL)
    for core, part in enumerate((own_ref, pair_ref)):
        rows = pl.ds(pl.multiple_of(spots[core] * half, half), half)
        total += dot(part[...], grads[rows, :], 1, 0)
    out_ref[...] = base_ref[...] + total.T


def input_product(spots, every, own, pair, base):
    rows, width = base.shape
    tile = 512
    weights = pl.BlockSpec((tile, own.shape[1]), lambda i, s: (i, 0))
    block = pl.BlockSpec((rows, tile), lambda i, s: (0, i))
    return pl.pallas_call(
        input_kernel,
        grid_spec=pltpu.PrefetchScalarGridSpec(
            num_scalar_prefetch=1,
            grid=(width // tile,),
            in_specs=[pl.BlockSpec(every.shape, lambda i, s: (0, 0, 0)), weights, weights, block],
            out_specs=block,
            scratch_shapes=[pltpu.VMEM((2 * own.shape[1], rows), LOW)],
        ),
        out_shape=jax.ShapeDtypeStruct((rows, width), FULL),
        compiler_params=pltpu.CompilerParams(vmem_limit_bytes=58 * 1024 * 1024),
        name="input_product",
    )(spots, every, own, pair, base)


def head_place(index):
    return (index // 4) * 4 + (index % 2) * 2 + (index // 2) % 2


def out_kernel(spots, att_ref, own_ref, pair_ref, x_ref, norms_ref, att_out_ref, low_ref, hid_ref,
               normal_ref, inverse_ref, rows_scratch, branch):
    for head in range(HEADS):
        rows_scratch[head * HEAD_DIM : (head + 1) * HEAD_DIM, :] = att_ref[head_place(head)]
    attended = rows_scratch[...].astype(FULL).T.astype(LOW)
    att_out_ref[...] = attended
    half = own_ref.shape[1]
    for core, part in enumerate((own_ref, pair_ref)):
        columns = pl.ds(pl.multiple_of(spots[core] * half, half), half)
        branch[:, columns] = dot(attended, part[...], 1, 0)
    residual = x_ref[...].astype(FULL) + branch[...]
    normal, inverse = norm_forward(residual)
    hidden = normal * norms_ref[0:1] + norms_ref[1:2]
    hid_ref[...] = hidden
    low_ref[...] = hidden.astype(LOW)
    normal_ref[...] = normal
    inverse_ref[...] = jnp.broadcast_to(inverse, (BLOCK, BLOCK))


def whole_specs(shapes):
    return [pl.BlockSpec(s, lambda i, p, n=len(s): (0,) * n) for s in shapes]


def local_call(kernel, spots, arrays, outs, scratch, name, limit=40):
    return pl.pallas_call(
        kernel,
        grid_spec=pltpu.PrefetchScalarGridSpec(
            num_scalar_prefetch=1,
            grid=(1,),
            in_specs=whole_specs([a.shape for a in arrays]),
            out_specs=whole_specs([o.shape for o in outs]),
            scratch_shapes=scratch,
        ),
        out_shape=outs,
        compiler_params=pltpu.CompilerParams(vmem_limit_bytes=limit * 1024 * 1024),
        name=name,
    )(spots, *arrays)


def out_and_norm(spots, blocks, out_halves, inputs, norms):
    rows, width = inputs.shape
    arrays = [blocks, *out_halves, inputs, norms]
    shape = jax.ShapeDtypeStruct
    return local_call(
        out_kernel,
        spots,
        arrays,
        [
            shape((rows, width), LOW),
            shape((rows, width), LOW),
            shape((rows, width), FULL),
            shape((rows, width), FULL),
            shape((rows, BLOCK), FULL),
        ],
        [pltpu.VMEM((width, rows), LOW), pltpu.VMEM((rows, width), FULL)],
        "out_and_norm",
        58,
    )


def norm_one_kernel(spots, base_ref, late_ref, normal_ref, inverse_ref, norms_ref, own_ref,
                    pair_ref, att_ref, grad_ref, pairs_ref, blocks_ref, sums_ref, total):
    grad = base_ref[...] + late_ref[...].astype(FULL)
    normal = normal_ref[...]
    result, gain_sum, bias_sum = norm_backward(grad, normal, inverse_ref[:, :1], norms_ref[0:1])
    grad_ref[...] = result
    low = result.astype(LOW)
    pairs_ref[: low.shape[0]] = low
    pairs_ref[low.shape[0] :] = att_ref[...]
    sums_ref[0:1, :] = gain_sum[None]
    sums_ref[1:2, :] = bias_sum[None]
    half = own_ref.shape[1]
    for core, part in enumerate((own_ref, pair_ref)):
        columns = pl.ds(pl.multiple_of(spots[core] * half, half), half)
        term = dot(part[...], pairs_ref[: low.shape[0], columns], 1, 1)
        total[...] = term if core == 0 else total[...] + term
    for head in range(HEADS):
        rows = slice(head * HEAD_DIM, (head + 1) * HEAD_DIM)
        blocks_ref[head_place(head)] = total[rows, :].astype(LOW)


def norm_one_back(spots, base, late, normal, inverse, norms, out_halves, attended_low):
    rows, width = base.shape
    arrays = [base, late, normal, inverse, norms, *out_halves, attended_low]
    shape = jax.ShapeDtypeStruct
    return local_call(
        norm_one_kernel,
        spots,
        arrays,
        [
            shape((rows, width), FULL),
            shape((2 * rows, width), LOW),
            shape((HEADS, HEAD_DIM, rows), LOW),
            shape((2, width), FULL),
        ],
        [pltpu.VMEM((width, rows), FULL)],
        "norm_one_back",
        58,
    )


def ff_terms_kernel(hid_a, hid_b, up_a, up_b, mixed_a, mixed_b, act_a, act_b, out_ref, left):
    step = pl.program_id(0)
    steps = pl.num_programs(0) // 2
    half = hid_a.shape[0]

    @pl.when(step == 0)
    def _():
        left[:, :half] = hid_a[...].astype(FULL).T.astype(LOW)
        left[:, half:] = hid_b[...].astype(FULL).T.astype(LOW)

    @pl.when(step == steps)
    def _():
        left[:, :half] = mixed_a[...].astype(FULL).T.astype(LOW)
        left[:, half:] = mixed_b[...].astype(FULL).T.astype(LOW)

    @pl.when(step < steps)
    def _():
        right = jnp.concatenate([up_a[...], up_b[...]], axis=0)
        out_ref[...] = dot(left[...], right, 1, 0).astype(LOW)

    @pl.when(step >= steps)
    def _():
        right = jnp.concatenate([act_a[...], act_b[...]], axis=0)
        out_ref[...] = dot(left[...], right, 1, 0).astype(LOW)


def ff_products(hidden, grad_upward, grad_mixed, activated):
    count, width = hidden[0].shape
    units = activated[0].shape[1]
    tile = 512
    steps = units // tile
    whole = pl.BlockSpec((count, width), lambda i: (0, 0))
    early = pl.BlockSpec((count, tile), lambda i: (0, jnp.minimum(i, steps - 1)))
    later = pl.BlockSpec((count, tile), lambda i: (0, jnp.maximum(i - steps, 0)))
    return pl.pallas_call(
        ff_terms_kernel,
        grid=(2 * steps,),
        in_specs=[whole, whole, early, early, whole, whole, later, later],
        out_specs=pl.BlockSpec((width, tile), lambda i: (0, i)),
        out_shape=jax.ShapeDtypeStruct((width, 2 * units), LOW),
        scratch_shapes=[pltpu.VMEM((width, 2 * count), LOW)],
        compiler_params=pltpu.CompilerParams(vmem_limit_bytes=58 * 1024 * 1024),
        cost_estimate=pl.CostEstimate(
            flops=8 * count * width * units, bytes_accessed=8 * width * units, transcendentals=0
        ),
        name="ff_products",
    )(*hidden, *grad_upward, *grad_mixed, *activated)


def norm_forward(values):
    center = values - jnp.mean(values, axis=-1, keepdims=True)
    spread = jnp.mean(center * center, axis=-1, keepdims=True)
    inverse = lax.rsqrt(spread + EPSILON)
    return center * inverse, inverse


def norm_backward(grad, normal, inverse, gain):
    scaled = grad * gain
    result = inverse * (
        scaled
        - jnp.mean(scaled, axis=-1, keepdims=True)
        - normal * jnp.mean(scaled * normal, axis=-1, keepdims=True)
    )
    return result, jnp.sum(grad * normal, axis=0), jnp.sum(grad, axis=0)


def gather_group(value, near_work, far_work):
    late = swap(value, "zl")
    near = with_pair(value, "core")
    late, near, *done = lax.optimization_barrier((late, near, *near_work(near)))
    far = with_pair(late, "core")
    return (near, far), list(zip(done, far_work(far)))


def product_group(parts, right, left_dim, right_dim):
    near, far = parts
    half = far.shape[0] // 2
    term = dot(far, right, left_dim, right_dim)
    sent = term[:half] + swap(term[half:].astype(LOW), "core").astype(FULL)
    sent, near = lax.optimization_barrier((sent.astype(LOW), near))
    late = swap(sent, "zl")
    term = dot(near, right, left_dim, right_dim)
    return term[:half] + swap(term[half:].astype(LOW), "core").astype(FULL), late, sent


def per_device(
    tokens, w_qkv, w_out, w_up, w_down, ln1_gain, ln1_bias, ln2_gain, ln2_bias, cotangent
):
    inputs = tokens[0]
    width = inputs.shape[1]
    units = w_up.shape[1]
    ff_part = units // 4
    out_part = width // 4
    z, zh, zl, xh, core = (lax.axis_index(a) for a in (Z, "zh", "zl", "xh", "core"))
    group = zl * 2 + core
    pair = z * 2 + core
    place = jnp.stack(
        [
            ((z ^ dz) * 2 + (xh ^ dx)) * 2 + (core ^ dc)
            for dx in range(2)
            for dc in range(2)
            for dz in (0, 1, 3, 2)
        ]
    ).astype(jnp.int32)
    cores = jnp.stack([core, 1 - core]).astype(jnp.int32)
    groups = jnp.stack(
        [(zl ^ dl) * 2 + (core ^ dc) for dc in range(2) for dl in range(2)]
    ).astype(jnp.int32)

    heads = [
        lax.dynamic_slice_in_dim(w_qkv, which * width + pair * BLOCK, BLOCK, 1) for which in range(3)
    ]
    first = jnp.concatenate([h[:, :HEAD_DIM] for h in heads], axis=1)
    second = jnp.concatenate([h[:, HEAD_DIM:] for h in heads], axis=1)
    own_mine = jnp.where(xh == 0, first, second)
    norm_rows = jnp.pad(
        jnp.stack([ln1_gain, ln1_bias, ln2_gain, ln2_bias]), ((0, 12), (0, BLOCK))
    )
    early = jnp.concatenate([jnp.pad(own_mine, ((0, 0), (0, HEAD_DIM))), norm_rows], axis=0)
    together = lax.optimization_barrier
    early, inputs = together((jnp.broadcast_to(early[None], (8,) + early.shape), inputs))
    early = lax.all_to_all(early, FSDP, split_axis=0, concat_axis=0, tiled=True)
    up_mine = lax.dynamic_slice_in_dim(w_up, group * ff_part, ff_part, 1)
    down_mine = lax.dynamic_slice_in_dim(w_down, group * ff_part, ff_part, 1)
    out_mine = lax.dynamic_slice_in_dim(w_out, core * (width // 2), width // 2, 1)
    rest = jnp.concatenate([up_mine, down_mine, out_mine], axis=1)
    rest = lax.all_gather(rest, FSDP, axis=0, tiled=True)
    far, one = together((swap(inputs, "xh"), exchange(inputs, Z, 1)))
    near_two = jnp.concatenate([inputs, one], axis=0)
    near_rest, far_one = together((exchange(near_two, Z, 3), exchange(far, Z, 1)))
    near_half, early = together((jnp.concatenate([near_two, near_rest], axis=0), early))
    far_two = jnp.concatenate([far, far_one], axis=0)
    far_rest = exchange(far_two, Z, 3)
    near_core = swap(near_half, "core")
    far_half = jnp.concatenate([far_two, far_rest], axis=0)
    parts = [near_half, near_core, far_half, swap(far_half, "core")]
    own_qkv = early[:, :BLOCK, : 3 * HEAD_DIM].reshape(width, 3 * HEAD_DIM)
    norms = early[:, BLOCK : BLOCK + 4, :BLOCK].astype(FULL).transpose(1, 0, 2).reshape(4, width)
    gain_two, bias_two = norms[2:3], norms[3:4]
    head = jnp.concatenate([dot(own_qkv, p, 0, 1).astype(LOW) for p in parts], axis=1)

    low_blocks, attended, log_total = attention_forward(place, head)
    low_blocks = lax.all_to_all(low_blocks, CTX, split_axis=0, concat_axis=0, tiled=True)
    qkv_mine = lax.dynamic_slice_in_dim(w_qkv, core * (3 * width // 2), 3 * width // 2, 1)
    qkv_mine, log_total = together((qkv_mine, log_total))
    rest, low_blocks = together((rest, low_blocks))
    out_mine = rest[:, 2 * ff_part :]
    out_halves = out_mine, swap(out_mine, "core")
    up_part = rest[:, :ff_part]
    down_part = rest[:, ff_part : 2 * ff_part]
    qkv_own = lax.all_gather(qkv_mine, FSDP, axis=0, tiled=True)
    attended_low, hidden_low, hidden, normal_one, inverse_one = out_and_norm(
        cores, low_blocks, out_halves, inputs, norms
    )

    def raise_part(rows):
        upward = dot(rows, up_part, 1, 0)
        cdf = 0.5 * (1.0 + lax.erf(upward * math.sqrt(0.5)))
        pdf = jnp.exp(-0.5 * upward * upward) * (1.0 / math.sqrt(2.0 * math.pi))
        return (upward * cdf).astype(LOW), cdf + upward * pdf

    hidden_low, (activated_low, slope) = gather_group(hidden_low, raise_part, raise_part)
    near, late, _ = product_group(activated_low, down_part, 1, 1)
    mixed = hidden + near + late.astype(FULL)
    normal_two, inverse_two = norm_forward(mixed)
    layer_out = (normal_two * gain_two + bias_two).astype(LOW)

    grad_mixed, gain_two_grad, bias_two_grad = norm_backward(
        cotangent[0].astype(FULL), normal_two, inverse_two, gain_two
    )
    lower_near, lower_far = (
        lambda rows, k=k: ((dot(rows, down_part, 1, 0) * k).astype(LOW),) for k in slope
    )
    grad_mixed_low, (grad_upward_low,) = gather_group(
        grad_mixed.astype(LOW), lower_near, lower_far
    )
    near, late, sent = product_group(grad_upward_low, up_part, 1, 1)
    near, *held = together((near, *hidden_low))
    ff_terms = ff_products(held, grad_upward_low, grad_mixed_low, activated_low)
    ff_share = lax.psum_scatter(ff_terms, FSDP, scatter_dimension=0, tiled=True)

    grad_residual, pairs, grad_blocks, norm_one_sums = norm_one_back(
        cores, grad_mixed + near, late, normal_one, inverse_one, norms, out_halves, attended_low
    )
    grad_blocks = lax.all_to_all(grad_blocks, CTX, split_axis=0, concat_axis=0, tiled=True)
    pairs, qkv_own = together((pairs, qkv_own))
    qkv_pair = swap(qkv_own, "core")
    late_pairs = swap(pairs, "zl")
    blocks = [pairs, swap(pairs, "core"), late_pairs, swap(late_pairs, "core")]

    grad_near, grad_far, grad_out = attention_backward(
        place, head, grad_blocks, attended, log_total
    )
    norm_two_sums = jnp.stack([gain_two_grad, bias_two_grad])
    terms = weight_terms(
        groups[:1], grad_near, grad_far, parts, blocks, norm_one_sums, norm_two_sums
    )
    shares = lax.all_to_all(terms, FSDP, split_axis=0, concat_axis=0, tiled=True)

    def sum_pair(value, axis):
        return (value.astype(FULL) + swap(value, axis).astype(FULL)).astype(LOW)

    size = 3 * HEAD_DIM
    def spread(qkv_part, out_part, axis):
        theirs = swap(jnp.concatenate([qkv_part, out_part], axis=0), axis)
        count = qkv_part.shape[0]
        summed = out_part.astype(FULL) + theirs[count:].astype(FULL)
        return jnp.concatenate([qkv_part, theirs[:count]], axis=0), summed.astype(LOW)

    ff_share, grad_out, shares = together((ff_share, grad_out, shares))
    every = lax.all_to_all(grad_out, CTX, split_axis=0, concat_axis=0, tiled=True)
    shares = jnp.sum(shares.astype(FULL), axis=0).astype(LOW)
    every, *sums = together((every, *spread(shares[:size], shares[size:], "xh")))
    sums = spread(*sums, "zh")
    ff_sum = sum_pair(sum_pair(ff_share, "zh"), "xh")
    ff_sum, every, *sums = together((ff_sum, every, *sums))
    input_grad = input_product(cores, every, qkv_own, qkv_pair, grad_residual)
    ff_sum, input_grad, rest_sum = together(
        (with_pair(ff_sum, "zl"), input_grad, with_pair(jnp.concatenate(sums, axis=0), "zl"))
    )
    ff_pair, rest_pair = swap(ff_sum, "core"), swap(rest_sum, "core")
    spots = [
        ((zh ^ dh) * 2 + (zl ^ dl)) * 2 + (core ^ dc)
        for dc in range(2)
        for dl in range(2)
        for dh in range(2)
    ]
    spots = jnp.concatenate([jnp.stack(spots).astype(jnp.int32), groups, xh[None].astype(jnp.int32)])
    grad_w_qkv, grad_w_out, norm_grads = assemble_rest(spots, rest_sum, rest_pair, width)
    grad_w_up, grad_w_down = assemble(groups, [ff_sum, ff_pair], units)

    return (
        layer_out[None],
        input_grad[None],
        grad_w_qkv,
        grad_w_out,
        grad_w_up,
        grad_w_down,
        norm_grads[0],
        norm_grads[1],
        norm_grads[2],
        norm_grads[3],
    )


def solution(mesh):
    fine = Mesh(mesh.devices.reshape(2, 2, 2, 2, 2, 4), ("zh", "zl", "xh", "core", "xl", "y"))
    block = P(FSDP, CTX, None)
    rows = P(FSDP, None)
    row = P(FSDP)
    return jax.shard_map(
        per_device,
        mesh=fine,
        in_specs=(block, rows, rows, rows, rows, row, row, row, row, block),
        out_specs=(block, block, rows, rows, rows, rows, row, row, row, row),
        check_vma=False,
    )
```

```python
import math

import jax
import jax.numpy as jnp
from jax import lax
from jax.experimental import pallas as pl
from jax.experimental.pallas import tpu as pltpu
from jax.sharding import Mesh, PartitionSpec as P

HEADS = 16
HEAD_DIM = 64
BLOCK = 128
EPSILON = 1e-12
LOW = jnp.bfloat16
FULL = jnp.float32

CTX = ("zh", "zl", "xh", "core")
FSDP = ("xl", "y")
Z = ("zh", "zl")
SCALE = HEAD_DIM**-0.5
QUERY_BLOCK = 256
FORWARD_BLOCK = 512
PARTS = QUERY_BLOCK // BLOCK


def dot(left, right, left_dim, right_dim):
    return lax.dot_general(
        left, right, (((left_dim,), (right_dim,)), ((), ())), preferred_element_type=FULL
    )


def swap(value, axis):
    return lax.ppermute(value, axis, [(0, 1), (1, 0)])


def exchange(value, axes, mask):
    return lax.ppermute(value, axes, [(i, i ^ mask) for i in range(4)])


def with_pair(value, axis):
    return jnp.concatenate([value, swap(value, axis)], axis=0)


def with_four(value, axes):
    moved = {mask: exchange(value, axes, mask) for mask in (1, 3, 2)}
    return jnp.concatenate([value, moved[1], moved[2], moved[3]], axis=0)


def forward_kernel(place, q_ref, k_ref, v_ref, low_ref, out_ref, log_ref, keys):
    step = pl.program_id(0)

    @pl.when(step == 0)
    def _():
        keys[...] = k_ref[...].astype(FULL).T.astype(LOW)

    queries = q_ref[...] * LOW(SCALE)
    scores = dot(keys[...], queries, 1, 0)
    top = jnp.max(scores, axis=0, keepdims=True)
    weights = jnp.exp(scores - top)
    total = jnp.sum(weights, axis=0, keepdims=True)
    attended = dot(v_ref[...], weights.astype(LOW), 1, 0) / total
    out_ref[...] = attended
    log_ref[...] = top + jnp.log(total)
    low = attended.astype(LOW)
    for part in range((FORWARD_BLOCK // BLOCK)):
        low_ref[place[step * (FORWARD_BLOCK // BLOCK) + part]] = low[:, part * BLOCK : (part + 1) * BLOCK]


def attention_forward(place, projected):
    length = projected.shape[1]
    return pl.pallas_call(
        forward_kernel,
        grid_spec=pltpu.PrefetchScalarGridSpec(
            num_scalar_prefetch=1,
            grid=(length // FORWARD_BLOCK,),
            in_specs=[
                pl.BlockSpec((HEAD_DIM, FORWARD_BLOCK), lambda i, p: (0, i)),
                pl.BlockSpec((HEAD_DIM, length), lambda i, p: (1, 0)),
                pl.BlockSpec((HEAD_DIM, length), lambda i, p: (2, 0)),
            ],
            out_specs=[
                pl.BlockSpec((length // BLOCK, HEAD_DIM, BLOCK), lambda i, p: (0, 0, 0)),
                pl.BlockSpec((HEAD_DIM, FORWARD_BLOCK), lambda i, p: (0, i)),
                pl.BlockSpec((1, FORWARD_BLOCK), lambda i, p: (0, i)),
            ],
            scratch_shapes=[pltpu.VMEM((length, HEAD_DIM), LOW)],
        ),
        out_shape=[
            jax.ShapeDtypeStruct((length // BLOCK, HEAD_DIM, BLOCK), LOW),
            jax.ShapeDtypeStruct((HEAD_DIM, length), FULL),
            jax.ShapeDtypeStruct((1, length), FULL),
        ],
        compiler_params=pltpu.CompilerParams(vmem_limit_bytes=40 * 1024 * 1024),
        cost_estimate=pl.CostEstimate(
            flops=16 * length * length * HEAD_DIM,
            bytes_accessed=10 * length * HEAD_DIM,
            transcendentals=length * length,
        ),
        name="attention_forward",
    )(place, projected, projected, projected)


def backward_kernel(
    place, q_ref, k_ref, v_ref, grad_ref, out_ref, log_ref, near_ref, far_ref, blocks_ref,
    keys, values, dk, dv,
):
    step = pl.program_id(0)

    @pl.when(step == 0)
    def _():
        keys[...] = k_ref[...].astype(FULL).T.astype(LOW)
        values[...] = v_ref[...].astype(FULL).T.astype(LOW)
        dk[...] = jnp.zeros_like(dk)
        dv[...] = jnp.zeros_like(dv)

    queries = q_ref[...] * LOW(SCALE)
    grad = jnp.concatenate([grad_ref[place[step * PARTS + p]] for p in range(PARTS)], axis=1)
    delta = jnp.sum(grad.astype(FULL) * out_ref[...], axis=0, keepdims=True)
    scores = dot(keys[...], queries, 1, 0)
    probs = jnp.exp(scores - log_ref[...])
    grad_probs = dot(values[...], grad, 1, 0)
    grad_scores = (probs * (grad_probs - delta)).astype(LOW)
    dv[...] += dot(grad, probs.astype(LOW), 1, 1)
    dk[...] += dot(queries, grad_scores, 1, 1)
    dq = (dot(k_ref[...], grad_scores, 1, 0) * SCALE).astype(LOW)
    steps = pl.num_programs(0)
    half = near_ref.shape[1]
    start = pl.multiple_of(lax.rem(step, steps // 2) * QUERY_BLOCK, QUERY_BLOCK)

    for part in range(PARTS):
        blocks_ref[place[step * PARTS + part], :HEAD_DIM] = dq[:, part * BLOCK : (part + 1) * BLOCK]

    @pl.when(step < steps // 2)
    def _():
        near_ref[:HEAD_DIM, pl.ds(start, QUERY_BLOCK)] = dq

    @pl.when(step >= steps // 2)
    def _():
        far_ref[:HEAD_DIM, pl.ds(start, QUERY_BLOCK)] = dq

    @pl.when(step == steps - 1)
    def _():
        for part, total in ((1, dk), (2, dv)):
            rows = slice(part * HEAD_DIM, (part + 1) * HEAD_DIM)
            near_ref[rows, :] = total[:, :half].astype(LOW)
            far_ref[rows, :] = total[:, half:].astype(LOW)
            for block in range(HEADS):
                blocks_ref[place[block], rows] = total[
                    :, block * BLOCK : (block + 1) * BLOCK
                ].astype(LOW)


def attention_backward(place, projected, grad_blocks, attended, log_total):
    length = projected.shape[1]
    half = jax.ShapeDtypeStruct((3 * HEAD_DIM, length // 2), LOW)
    blocks = jax.ShapeDtypeStruct((length // BLOCK, 3 * HEAD_DIM, BLOCK), LOW)
    return pl.pallas_call(
        backward_kernel,
        grid_spec=pltpu.PrefetchScalarGridSpec(
            num_scalar_prefetch=1,
            grid=(length // QUERY_BLOCK,),
            in_specs=[
                pl.BlockSpec((HEAD_DIM, QUERY_BLOCK), lambda i, p: (0, i)),
                pl.BlockSpec((HEAD_DIM, length), lambda i, p: (1, 0)),
                pl.BlockSpec((HEAD_DIM, length), lambda i, p: (2, 0)),
                pl.BlockSpec((length // BLOCK, HEAD_DIM, BLOCK), lambda i, p: (0, 0, 0)),
                pl.BlockSpec((HEAD_DIM, QUERY_BLOCK), lambda i, p: (0, i)),
                pl.BlockSpec((1, QUERY_BLOCK), lambda i, p: (0, i)),
            ],
            out_specs=[pl.BlockSpec(half.shape, lambda i, p: (0, 0))] * 2
            + [pl.BlockSpec(blocks.shape, lambda i, p: (0, 0, 0))],
            scratch_shapes=[
                pltpu.VMEM((length, HEAD_DIM), LOW),
                pltpu.VMEM((length, HEAD_DIM), LOW),
                pltpu.VMEM((HEAD_DIM, length), FULL),
                pltpu.VMEM((HEAD_DIM, length), FULL),
            ],
        ),
        out_shape=[half, half, blocks],
        compiler_params=pltpu.CompilerParams(vmem_limit_bytes=58 * 1024 * 1024),
        cost_estimate=pl.CostEstimate(
            flops=40 * length * length * HEAD_DIM,
            bytes_accessed=20 * length * HEAD_DIM,
            transcendentals=length * length,
        ),
        name="attention_backward",
    )(place, projected, projected, projected, grad_blocks, attended, log_total)


def assemble_kernel(spots, own_ref, pair_ref, up_ref, down_ref):
    part = up_ref.shape[1] // 4
    rows = up_ref.shape[0]
    for core, piece in enumerate((own_ref, pair_ref)):
        for zl in range(2):
            lane = pl.multiple_of(spots[core * 2 + zl] * part, part)
            source = slice(zl * rows, (zl + 1) * rows)
            up_ref[:, pl.ds(lane, part)] = piece[source, :part].astype(FULL)
            down_ref[:, pl.ds(lane, part)] = piece[source, part:].astype(FULL)


def assemble(spots, pieces, units):
    shape = jax.ShapeDtypeStruct((BLOCK, units), FULL)
    return local_call(assemble_kernel, spots, pieces, [shape, shape], [], "assemble")


def terms_kernel(spots, near_ref, far_ref, part_0, part_1, part_2, part_3, block_0, block_1, block_2,
                 block_3, first_ref, second_ref, out_ref, total):
    size = near_ref.shape[0]
    count = part_0.shape[0]
    length = near_ref.shape[1]
    columns = out_ref.shape[1] - size - 16
    lanes = pl.ds(pl.multiple_of(spots[0] * columns, columns), columns)
    out = jnp.zeros((columns, length), FULL)
    for block in (block_0, block_1, block_2, block_3):
        out += dot(block[:BLOCK, lanes].astype(FULL).T.astype(LOW), block[BLOCK:], 1, 0)
    total[...] = jnp.zeros_like(total)
    for index, part in enumerate((part_0, part_1, part_2, part_3)):
        source = (near_ref, far_ref)[index // 2]
        start = index % 2 * count
        total[...] += dot(source[:, start : start + count], part[...], 1, 0)
    for block in range(out_ref.shape[0]):
        rows = slice(block * BLOCK, (block + 1) * BLOCK)
        out_ref[block, :size] = total[:, rows].astype(LOW)
        out_ref[block, size : size + columns] = out[:, rows].astype(LOW)
        norms = jnp.concatenate(
            [first_ref[:, rows], second_ref[:, rows], jnp.zeros((12, BLOCK), FULL)], axis=0
        )
        out_ref[block, size + columns :] = norms.astype(LOW)


def weight_terms(spots, near, far, parts, blocks, first, second):
    size, length = near.shape
    columns = length // 4
    outs = [jax.ShapeDtypeStruct((length // BLOCK, size + columns + 16, BLOCK), LOW)]
    arrays = [near, far, *parts, *blocks, first, second]
    scratch = [pltpu.VMEM((size, length), FULL)]
    return local_call(terms_kernel, spots, arrays, outs, scratch, "weight_terms")[0]


def assemble_rest_kernel(spots, own_ref, pair_ref, qkv_ref, out_ref, norm_ref):
    width = out_ref.shape[1]
    part = width // 4
    size = 3 * HEAD_DIM
    step = own_ref.shape[0] // 2
    flip = spots[12] == 1
    total = jnp.zeros((16, BLOCK), FULL)
    for core, piece in enumerate((own_ref, pair_ref)):
        for zl in range(2):
            for zh in range(2):
                start = zl * step + zh * 2 * size
                lane = spots[(core * 2 + zl) * 2 + zh] * BLOCK
                near = piece[start : start + size].astype(FULL)
                far = piece[start + size : start + 2 * size].astype(FULL)
                first = jnp.where(flip, far, near)
                second = jnp.where(flip, near, far)
                for which in range(3):
                    rows = slice(which * HEAD_DIM, (which + 1) * HEAD_DIM)
                    columns = pl.ds(pl.multiple_of(which * width + lane, BLOCK), BLOCK)
                    qkv_ref[:, columns] = jnp.concatenate([first[rows], second[rows]], axis=0).T
            start = zl * step + 4 * size
            lane = pl.multiple_of(spots[8 + core * 2 + zl] * part, part)
            out_ref[:, pl.ds(lane, part)] = piece[start : start + part].astype(FULL).T
            total += piece[start + part : start + part + 16].astype(FULL)
    norm_ref[...] = total


def assemble_rest(spots, own, pair, width):
    outs = [
        jax.ShapeDtypeStruct((BLOCK, 3 * width), FULL),
        jax.ShapeDtypeStruct((BLOCK, width), FULL),
        jax.ShapeDtypeStruct((16, BLOCK), FULL),
    ]
    return local_call(assemble_rest_kernel, spots, [own, pair], outs, [], "assemble_rest")


def input_kernel(spots, every_ref, own_ref, pair_ref, base_ref, out_ref, grads):
    half = own_ref.shape[1]

    @pl.when(pl.program_id(0) == 0)
    def _():
        for which in range(3):
            for head in range(HEADS):
                start = (which * HEADS + head) * HEAD_DIM
                grads[start : start + HEAD_DIM, :] = every_ref[
                    head_place(head), which * HEAD_DIM : (which + 1) * HEAD_DIM
                ]

    total = jnp.zeros((own_ref.shape[0], BLOCK), FULL)
    for core, part in enumerate((own_ref, pair_ref)):
        rows = pl.ds(pl.multiple_of(spots[core] * half, half), half)
        total += dot(part[...], grads[rows, :], 1, 0)
    out_ref[...] = base_ref[...] + total.T


def input_product(spots, every, own, pair, base):
    rows, width = base.shape
    tile = 512
    weights = pl.BlockSpec((tile, own.shape[1]), lambda i, s: (i, 0))
    block = pl.BlockSpec((rows, tile), lambda i, s: (0, i))
    return pl.pallas_call(
        input_kernel,
        grid_spec=pltpu.PrefetchScalarGridSpec(
            num_scalar_prefetch=1,
            grid=(width // tile,),
            in_specs=[pl.BlockSpec(every.shape, lambda i, s: (0, 0, 0)), weights, weights, block],
            out_specs=block,
            scratch_shapes=[pltpu.VMEM((2 * own.shape[1], rows), LOW)],
        ),
        out_shape=jax.ShapeDtypeStruct((rows, width), FULL),
        compiler_params=pltpu.CompilerParams(vmem_limit_bytes=58 * 1024 * 1024),
        name="input_product",
    )(spots, every, own, pair, base)


def head_place(index):
    return (index // 4) * 4 + (index % 2) * 2 + (index // 2) % 2


def out_kernel(spots, att_ref, own_ref, pair_ref, x_ref, norms_ref, att_out_ref, low_ref, hid_ref,
               normal_ref, inverse_ref, rows_scratch, branch):
    for head in range(HEADS):
        rows_scratch[head * HEAD_DIM : (head + 1) * HEAD_DIM, :] = att_ref[head_place(head)]
    attended = rows_scratch[...].astype(FULL).T.astype(LOW)
    att_out_ref[...] = attended
    half = own_ref.shape[1]
    for core, part in enumerate((own_ref, pair_ref)):
        columns = pl.ds(pl.multiple_of(spots[core] * half, half), half)
        branch[:, columns] = dot(attended, part[...], 1, 0)
    residual = x_ref[...].astype(FULL) + branch[...]
    normal, inverse = norm_forward(residual)
    hidden = normal * norms_ref[0:1] + norms_ref[1:2]
    hid_ref[...] = hidden
    low_ref[...] = hidden.astype(LOW)
    normal_ref[...] = normal
    inverse_ref[...] = jnp.broadcast_to(inverse, (BLOCK, BLOCK))


def whole_specs(shapes):
    return [pl.BlockSpec(s, lambda i, p, n=len(s): (0,) * n) for s in shapes]


def local_call(kernel, spots, arrays, outs, scratch, name, limit=40):
    return pl.pallas_call(
        kernel,
        grid_spec=pltpu.PrefetchScalarGridSpec(
            num_scalar_prefetch=1,
            grid=(1,),
            in_specs=whole_specs([a.shape for a in arrays]),
            out_specs=whole_specs([o.shape for o in outs]),
            scratch_shapes=scratch,
        ),
        out_shape=outs,
        compiler_params=pltpu.CompilerParams(vmem_limit_bytes=limit * 1024 * 1024),
        name=name,
    )(spots, *arrays)


def out_and_norm(spots, blocks, out_halves, inputs, norms):
    rows, width = inputs.shape
    arrays = [blocks, *out_halves, inputs, norms]
    shape = jax.ShapeDtypeStruct
    return local_call(
        out_kernel,
        spots,
        arrays,
        [
            shape((rows, width), LOW),
            shape((rows, width), LOW),
            shape((rows, width), FULL),
            shape((rows, width), FULL),
            shape((rows, BLOCK), FULL),
        ],
        [pltpu.VMEM((width, rows), LOW), pltpu.VMEM((rows, width), FULL)],
        "out_and_norm",
        58,
    )


def norm_one_kernel(spots, base_ref, late_ref, normal_ref, inverse_ref, norms_ref, own_ref,
                    pair_ref, att_ref, grad_ref, pairs_ref, blocks_ref, sums_ref, total):
    grad = base_ref[...] + late_ref[...].astype(FULL)
    normal = normal_ref[...]
    result, gain_sum, bias_sum = norm_backward(grad, normal, inverse_ref[:, :1], norms_ref[0:1])
    grad_ref[...] = result
    low = result.astype(LOW)
    pairs_ref[: low.shape[0]] = low
    pairs_ref[low.shape[0] :] = att_ref[...]
    sums_ref[0:1, :] = gain_sum[None]
    sums_ref[1:2, :] = bias_sum[None]
    half = own_ref.shape[1]
    for core, part in enumerate((own_ref, pair_ref)):
        columns = pl.ds(pl.multiple_of(spots[core] * half, half), half)
        term = dot(part[...], pairs_ref[: low.shape[0], columns], 1, 1)
        total[...] = term if core == 0 else total[...] + term
    for head in range(HEADS):
        rows = slice(head * HEAD_DIM, (head + 1) * HEAD_DIM)
        blocks_ref[head_place(head)] = total[rows, :].astype(LOW)


def norm_one_back(spots, base, late, normal, inverse, norms, out_halves, attended_low):
    rows, width = base.shape
    arrays = [base, late, normal, inverse, norms, *out_halves, attended_low]
    shape = jax.ShapeDtypeStruct
    return local_call(
        norm_one_kernel,
        spots,
        arrays,
        [
            shape((rows, width), FULL),
            shape((2 * rows, width), LOW),
            shape((HEADS, HEAD_DIM, rows), LOW),
            shape((2, width), FULL),
        ],
        [pltpu.VMEM((width, rows), FULL)],
        "norm_one_back",
        58,
    )


def ff_terms_kernel(hid_a, hid_b, up_a, up_b, mixed_a, mixed_b, act_a, act_b, out_ref, left):
    step = pl.program_id(0)
    steps = pl.num_programs(0) // 2
    half = hid_a.shape[0]

    @pl.when(step == 0)
    def _():
        left[:, :half] = hid_a[...].astype(FULL).T.astype(LOW)
        left[:, half:] = hid_b[...].astype(FULL).T.astype(LOW)

    @pl.when(step == steps)
    def _():
        left[:, :half] = mixed_a[...].astype(FULL).T.astype(LOW)
        left[:, half:] = mixed_b[...].astype(FULL).T.astype(LOW)

    @pl.when(step < steps)
    def _():
        right = jnp.concatenate([up_a[...], up_b[...]], axis=0)
        out_ref[...] = dot(left[...], right, 1, 0).astype(LOW)

    @pl.when(step >= steps)
    def _():
        right = jnp.concatenate([act_a[...], act_b[...]], axis=0)
        out_ref[...] = dot(left[...], right, 1, 0).astype(LOW)


def ff_products(hidden, grad_upward, grad_mixed, activated):
    count, width = hidden[0].shape
    units = activated[0].shape[1]
    tile = 512
    steps = units // tile
    whole = pl.BlockSpec((count, width), lambda i: (0, 0))
    early = pl.BlockSpec((count, tile), lambda i: (0, jnp.minimum(i, steps - 1)))
    later = pl.BlockSpec((count, tile), lambda i: (0, jnp.maximum(i - steps, 0)))
    return pl.pallas_call(
        ff_terms_kernel,
        grid=(2 * steps,),
        in_specs=[whole, whole, early, early, whole, whole, later, later],
        out_specs=pl.BlockSpec((width, tile), lambda i: (0, i)),
        out_shape=jax.ShapeDtypeStruct((width, 2 * units), LOW),
        scratch_shapes=[pltpu.VMEM((width, 2 * count), LOW)],
        compiler_params=pltpu.CompilerParams(vmem_limit_bytes=58 * 1024 * 1024),
        cost_estimate=pl.CostEstimate(
            flops=8 * count * width * units, bytes_accessed=8 * width * units, transcendentals=0
        ),
        name="ff_products",
    )(*hidden, *grad_upward, *grad_mixed, *activated)


def norm_forward(values):
    center = values - jnp.mean(values, axis=-1, keepdims=True)
    spread = jnp.mean(center * center, axis=-1, keepdims=True)
    inverse = lax.rsqrt(spread + EPSILON)
    return center * inverse, inverse


def norm_backward(grad, normal, inverse, gain):
    scaled = grad * gain
    result = inverse * (
        scaled
        - jnp.mean(scaled, axis=-1, keepdims=True)
        - normal * jnp.mean(scaled * normal, axis=-1, keepdims=True)
    )
    return result, jnp.sum(grad * normal, axis=0), jnp.sum(grad, axis=0)


def gather_group(value, near_work, far_work):
    late = swap(value, "zl")
    near = with_pair(value, "core")
    late, near, *done = lax.optimization_barrier((late, near, *near_work(near)))
    far = with_pair(late, "core")
    return (near, far), list(zip(done, far_work(far)))


def product_group(parts, right, left_dim, right_dim):
    near, far = parts
    half = far.shape[0] // 2
    term = dot(far, right, left_dim, right_dim)
    sent = term[:half] + swap(term[half:].astype(LOW), "core").astype(FULL)
    sent, near = lax.optimization_barrier((sent.astype(LOW), near))
    late = swap(sent, "zl")
    term = dot(near, right, left_dim, right_dim)
    return term[:half] + swap(term[half:].astype(LOW), "core").astype(FULL), late, sent


def per_device(
    tokens, w_qkv, w_out, w_up, w_down, ln1_gain, ln1_bias, ln2_gain, ln2_bias, cotangent
):
    inputs = tokens[0]
    width = inputs.shape[1]
    units = w_up.shape[1]
    ff_part = units // 4
    out_part = width // 4
    z, zh, zl, xh, core = (lax.axis_index(a) for a in (Z, "zh", "zl", "xh", "core"))
    group = zl * 2 + core
    pair = z * 2 + core
    place = jnp.stack(
        [
            ((z ^ dz) * 2 + (xh ^ dx)) * 2 + (core ^ dc)
            for dx in range(2)
            for dc in range(2)
            for dz in (0, 1, 3, 2)
        ]
    ).astype(jnp.int32)
    cores = jnp.stack([core, 1 - core]).astype(jnp.int32)
    groups = jnp.stack(
        [(zl ^ dl) * 2 + (core ^ dc) for dc in range(2) for dl in range(2)]
    ).astype(jnp.int32)

    heads = [
        lax.dynamic_slice_in_dim(w_qkv, which * width + pair * BLOCK, BLOCK, 1) for which in range(3)
    ]
    first = jnp.concatenate([h[:, :HEAD_DIM] for h in heads], axis=1)
    second = jnp.concatenate([h[:, HEAD_DIM:] for h in heads], axis=1)
    own_mine = jnp.where(xh == 0, first, second)
    norm_rows = jnp.pad(
        jnp.stack([ln1_gain, ln1_bias, ln2_gain, ln2_bias]), ((0, 12), (0, BLOCK))
    )
    early = jnp.concatenate([jnp.pad(own_mine, ((0, 0), (0, HEAD_DIM))), norm_rows], axis=0)
    together = lax.optimization_barrier
    early, inputs = together((jnp.broadcast_to(early[None], (8,) + early.shape), inputs))
    early = lax.all_to_all(early, FSDP, split_axis=0, concat_axis=0, tiled=True)
    up_mine = lax.dynamic_slice_in_dim(w_up, group * ff_part, ff_part, 1)
    down_mine = lax.dynamic_slice_in_dim(w_down, group * ff_part, ff_part, 1)
    out_mine = lax.dynamic_slice_in_dim(w_out, core * (width // 2), width // 2, 1)
    rest = jnp.concatenate([up_mine, down_mine, out_mine], axis=1)
    rest = lax.all_gather(rest, FSDP, axis=0, tiled=True)
    far, one = together((swap(inputs, "xh"), exchange(inputs, Z, 1)))
    near_two = jnp.concatenate([inputs, one], axis=0)
    near_rest, far_one = together((exchange(near_two, Z, 3), exchange(far, Z, 1)))
    near_half, early = together((jnp.concatenate([near_two, near_rest], axis=0), early))
    far_two = jnp.concatenate([far, far_one], axis=0)
    far_rest = exchange(far_two, Z, 3)
    near_core = swap(near_half, "core")
    far_half = jnp.concatenate([far_two, far_rest], axis=0)
    parts = [near_half, near_core, far_half, swap(far_half, "core")]
    own_qkv = early[:, :BLOCK, : 3 * HEAD_DIM].reshape(width, 3 * HEAD_DIM)
    norms = early[:, BLOCK : BLOCK + 4, :BLOCK].astype(FULL).transpose(1, 0, 2).reshape(4, width)
    gain_two, bias_two = norms[2:3], norms[3:4]
    head = jnp.concatenate([dot(own_qkv, p, 0, 1).astype(LOW) for p in parts], axis=1)

    low_blocks, attended, log_total = attention_forward(place, head)
    low_blocks = lax.all_to_all(low_blocks, CTX, split_axis=0, concat_axis=0, tiled=True)
    qkv_mine = lax.dynamic_slice_in_dim(w_qkv, core * (3 * width // 2), 3 * width // 2, 1)
    qkv_mine, log_total = together((qkv_mine, log_total))
    rest, low_blocks = together((rest, low_blocks))
    out_mine = rest[:, 2 * ff_part :]
    out_halves = out_mine, swap(out_mine, "core")
    up_part = rest[:, :ff_part]
    down_part = rest[:, ff_part : 2 * ff_part]
    qkv_own = lax.all_gather(qkv_mine, FSDP, axis=0, tiled=True)
    attended_low, hidden_low, hidden, normal_one, inverse_one = out_and_norm(
        cores, low_blocks, out_halves, inputs, norms
    )

    def raise_part(rows):
        upward = dot(rows, up_part, 1, 0)
        cdf = 0.5 * (1.0 + lax.erf(upward * math.sqrt(0.5)))
        pdf = jnp.exp(-0.5 * upward * upward) * (1.0 / math.sqrt(2.0 * math.pi))
        return (upward * cdf).astype(LOW), cdf + upward * pdf

    hidden_low, (activated_low, slope) = gather_group(hidden_low, raise_part, raise_part)
    near, late, _ = product_group(activated_low, down_part, 1, 1)
    mixed = hidden + near + late.astype(FULL)
    normal_two, inverse_two = norm_forward(mixed)
    layer_out = (normal_two * gain_two + bias_two).astype(LOW)

    grad_mixed, gain_two_grad, bias_two_grad = norm_backward(
        cotangent[0].astype(FULL), normal_two, inverse_two, gain_two
    )
    lower_near, lower_far = (
        lambda rows, k=k: ((dot(rows, down_part, 1, 0) * k).astype(LOW),) for k in slope
    )
    grad_mixed_low, (grad_upward_low,) = gather_group(
        grad_mixed.astype(LOW), lower_near, lower_far
    )
    near, late, sent = product_group(grad_upward_low, up_part, 1, 1)
    near, *held = together((near, *hidden_low))
    ff_terms = ff_products(held, grad_upward_low, grad_mixed_low, activated_low)
    ff_share = lax.psum_scatter(ff_terms, FSDP, scatter_dimension=0, tiled=True)

    grad_residual, pairs, grad_blocks, norm_one_sums = norm_one_back(
        cores, grad_mixed + near, late, normal_one, inverse_one, norms, out_halves, attended_low
    )
    grad_blocks = lax.all_to_all(grad_blocks, CTX, split_axis=0, concat_axis=0, tiled=True)
    pairs, qkv_own = together((pairs, qkv_own))
    qkv_pair = swap(qkv_own, "core")
    late_pairs = swap(pairs, "zl")
    blocks = [pairs, swap(pairs, "core"), late_pairs, swap(late_pairs, "core")]

    grad_near, grad_far, grad_out = attention_backward(
        place, head, grad_blocks, attended, log_total
    )
    norm_two_sums = jnp.stack([gain_two_grad, bias_two_grad])
    terms = weight_terms(
        groups[:1], grad_near, grad_far, parts, blocks, norm_one_sums, norm_two_sums
    )
    shares = lax.all_to_all(terms, FSDP, split_axis=0, concat_axis=0, tiled=True)

    def sum_pair(value, axis):
        return (value.astype(FULL) + swap(value, axis).astype(FULL)).astype(LOW)

    size = 3 * HEAD_DIM
    def spread(qkv_part, out_part, axis):
        theirs = swap(jnp.concatenate([qkv_part, out_part], axis=0), axis)
        count = qkv_part.shape[0]
        summed = out_part.astype(FULL) + theirs[count:].astype(FULL)
        return jnp.concatenate([qkv_part, theirs[:count]], axis=0), summed.astype(LOW)

    ff_share, grad_out, shares = together((ff_share, grad_out, shares))
    every = lax.all_to_all(grad_out, CTX, split_axis=0, concat_axis=0, tiled=True)
    shares = jnp.sum(shares.astype(FULL), axis=0).astype(LOW)
    every, *sums = together((every, *spread(shares[:size], shares[size:], "xh")))
    sums = spread(*sums, "zh")
    ff_sum = sum_pair(sum_pair(ff_share, "zh"), "xh")
    ff_sum, every, *sums = together((ff_sum, every, *sums))
    input_grad = input_product(cores, every, qkv_own, qkv_pair, grad_residual)
    ff_sum, input_grad, rest_sum = together(
        (with_pair(ff_sum, "zl"), input_grad, with_pair(jnp.concatenate(sums, axis=0), "zl"))
    )
    ff_pair, rest_pair = swap(ff_sum, "core"), swap(rest_sum, "core")
    spots = [
        ((zh ^ dh) * 2 + (zl ^ dl)) * 2 + (core ^ dc)
        for dc in range(2)
        for dl in range(2)
        for dh in range(2)
    ]
    spots = jnp.concatenate([jnp.stack(spots).astype(jnp.int32), groups, xh[None].astype(jnp.int32)])
    grad_w_qkv, grad_w_out, norm_grads = assemble_rest(spots, rest_sum, rest_pair, width)
    grad_w_up, grad_w_down = assemble(groups, [ff_sum, ff_pair], units)

    return (
        layer_out[None],
        input_grad[None],
        grad_w_qkv,
        grad_w_out,
        grad_w_up,
        grad_w_down,
        norm_grads[0],
        norm_grads[1],
        norm_grads[2],
        norm_grads[3],
    )


def solution(mesh):
    fine = Mesh(mesh.devices.reshape(2, 2, 2, 2, 2, 4), ("zh", "zl", "xh", "core", "xl", "y"))
    block = P(FSDP, CTX, None)
    rows = P(FSDP, None)
    row = P(FSDP)
    return jax.shard_map(
        per_device,
        mesh=fine,
        in_specs=(block, rows, rows, rows, rows, row, row, row, row, block),
        out_specs=(block, block, rows, rows, rows, rows, row, row, row, row),
        check_vma=False,
    )
```
